256 devices in a mesh: disp: 16 (over y, x_hi, core), col: 16 (over z, x_lo).
Axes of the slice: x: 4 (x_hi: 2, x_lo: 2; x = x_hi * 2 + x_lo), y: 4, z: 8, core: 2. Of those that a mesh axis runs over, the one named last changes fastest.
Arguments:
- left_feat: bfloat16 [320, 2, 4096], P('disp', None, 'col'), may hold values from -6 to 6
- right_feat: bfloat16 [320, 2, 4096], P('disp', None, 'col'), may hold values from -6 to 6
- conv1_w: bfloat16 [32, 40, 3, 3, 3], replicated, may hold values from -0.25 to 0.25
- conv2_w: bfloat16 [32, 32, 3, 3, 3], replicated, may hold values from -0.3125 to 0.3125
- conv3_w: bfloat16 [32, 32, 3, 3, 3], replicated, may hold values from -0.3125 to 0.3125
- head_w: float32 [32], replicated, may hold values from -120 to 120
Outputs:
- warped: bfloat16 [320, 2, 4096], P('disp', None, 'col')
- disparity: float32 [2, 4096], P(None, 'col')
The draws below stay inside these ranges and needn't reach their ends.
All inputs are finite; a program needn't handle non-finite values.
Results may differ from the reference program's by a relative error of at most 0.015.
The reference program's roundings to bfloat16 on the way count: a program that leaves them out, or rounds other values in their place, can miss the bound.
Values may be sent and summed in bfloat16 or wider, within the bound.
A program may use at most 64 MiB of HBM per device.

```python
import jax
import jax.numpy as jnp
from jax import lax

C = 320
G = 40
F = 32
H = 2
CG = 8
DISP = 256
W = 4096


def draw_head_w(key, part):
    values = jnp.clip(2.0 * jax.random.normal(key, (F,), jnp.float32), -8.0, 8.0)
    return values


def shard_levels(stream_key, dims, cuts, smallest, high):
    gain, own = 1.0, jax.random.fold_in(stream_key, 6)
    for position, shards_of in cuts:
        draws = jnp.exp(jax.random.uniform(jax.random.fold_in(own, position), (shards_of,), jnp.float32, smallest / len(cuts), high / len(cuts)))
        gain = gain * jnp.repeat(draws, dims[position] // shards_of).reshape([-1 if axis == position else 1 for axis in range(len(dims))])
    return gain


def normal_values(own_key, shape, deviation, bound, shards=(), kind=jnp.bfloat16):
    level = shard_levels(own_key, shape, shards, -0.22, 0.18) if shards else 1.0
    entries = jax.random.normal(own_key, shape, jnp.float32) * deviation * level
    return jnp.minimum(jnp.maximum(entries, -bound), bound).astype(kind)


def setup_inputs(seed: int = 0) -> dict:
    key_of = jax.random.split(jax.random.key(seed), 7)
    return {
        "left_feat": normal_values(key_of[0], (C, H, W), 1.0, 6.0, ((0, 16), (2, 16))),
        "right_feat": normal_values(key_of[1], (C, H, W), 1.0, 6.0, ((0, 16), (2, 16))),
        "conv1_w": normal_values(key_of[2], (F, G, 3, 3, 3), (G * 27 // 2) ** -0.5, 0.25),
        "conv2_w": normal_values(key_of[3], (F, F, 3, 3, 3), (F * 27 // 2) ** -0.5, 0.3125),
        "conv3_w": normal_values(key_of[4], (F, F, 3, 3, 3), (F * 27 // 2) ** -0.5, 0.3125),
        "head_w": draw_head_w(jax.random.fold_in(key_of[6], 71), 0),
    }


masked_value = -1.0e30


def convolve(activity, kernel):
    output = lax.conv_general_dilated(activity[None], kernel, (1, 1, 1), "SAME", dimension_numbers=("NCDHW", "OIDHW", "NCDHW"), preferred_element_type=jnp.float32)
    return jnp.maximum(output[0], 0.0)


def reference(left_feat, right_feat, conv1_w, conv2_w, conv3_w, head_w):
    padded_right = jnp.concatenate([jnp.zeros((C, H, DISP), right_feat.dtype), right_feat], axis=2)

    def correlate(offset):
        shifted = lax.dynamic_slice_in_dim(padded_right, (DISP - offset).astype(jnp.int32), W, 2)
        product = left_feat.astype(jnp.float32) * shifted.astype(jnp.float32)
        return (jnp.sum(product.reshape(G, CG, H, W), axis=1) / CG).astype(jnp.bfloat16)

    volume = jnp.moveaxis(lax.map(correlate, jnp.arange(DISP, dtype=jnp.int32)), 0, 1)
    activity = convolve(volume, conv1_w).astype(jnp.bfloat16)
    activity = convolve(activity, conv2_w).astype(jnp.bfloat16)
    activity = convolve(activity, conv3_w)
    scores = jnp.sum(head_w[:, None, None, None] * activity, axis=0)
    valid_mask = jnp.arange(W)[None, None, :] >= jnp.arange(DISP)[:, None, None]
    scores = jnp.where(valid_mask, scores, masked_value)
    top_score = jnp.max(scores, axis=0)
    weighting = jnp.where(valid_mask, jnp.exp(scores - top_score[None]), 0.0)
    denominator = jnp.sum(weighting, axis=0)
    disp_values = jnp.arange(DISP).astype(jnp.float32)[:, None, None]
    disp_sum = jnp.sum(weighting * disp_values, axis=0)

    def add_term(offset, running):
        shifted = lax.dynamic_slice_in_dim(padded_right, (DISP - offset).astype(jnp.int32), W, 2)
        weight = lax.dynamic_index_in_dim(weighting, offset, 0, keepdims=False)
        return running + weight[None] * shifted.astype(jnp.float32)

    numerator = lax.fori_loop(0, DISP, add_term, jnp.zeros((C, H, W), jnp.float32))
    warped = (numerator / denominator[None]).astype(jnp.bfloat16)
    return (warped, disp_sum / denominator / DISP)
```

```python
import jax
import jax.numpy as jnp
from jax import lax
from jax.experimental import pallas as pl
from jax.experimental.pallas import tpu as pltpu
from jax.sharding import PartitionSpec as P

N = 16
LANES = 128
DISP = 256
CH_ROWS = 40
WIDE_ROWS = 48
COLS0, COLS1, COLS2, COLS3 = 22, 20, 18, 16
F = 32
MASKED = -1e30
MESH = pl.DeviceIdType.MESH
NT = (((1,), (1,)), ((), ()))


def first_block(i):
    return lax.div(i + 7, 8) - 1


def places(block):
    for low, high, first in ((0, 0, -1), (1, 8, 0), (9, 15, 1)):
        slot = block - first
        if 0 <= slot < 4:
            yield slot, max(low, 7) if slot == 3 and high == 8 else low, high


def gather_kernel(own, wide, near, send_sem, recv_sem):
    i, j = lax.axis_index("disp"), lax.axis_index("col")
    base = first_block(i)

    def slot_filled(q):
        block = 2 * (j - 1) + base + q
        filled = (block >= 0) & (block < 2 * N)
        if q == 3:
            filled = filled & ((lax.rem(i, 8) == 0) | (lax.rem(i, 8) == 7))
        return filled

    slots = [wide.at[0], wide.at[1], near.at[0], near.at[1]]
    for q in range(4):

        @pl.when(jnp.logical_not(slot_filled(q)))
        def _(q=q):
            slots[q][...] = jnp.zeros(slots[q].shape, jnp.bfloat16)

    barrier = pltpu.get_barrier_semaphore()

    def greet(di, dj):
        pl.semaphore_signal(barrier, inc=1, device_id=(di, dj), device_id_type=MESH)

    def greet_strip(dj):
        @pl.loop(0, N)
        def _(step):
            greet(lax.rem(i + step, N), dj)

    @pl.loop(1, N)
    def _(step):
        greet(lax.rem(i + step, N), j)

    pl.when(j >= 1)(lambda: greet_strip(j - 1))
    pl.when((i == 0) & (j >= 2))(lambda: greet_strip(j - 2))
    pl.when((i == N - 1) & (j <= N - 2))(lambda: greet_strip(j + 1))
    targets = N - 1 + N * (j <= N - 2) + (j <= N - 3) + (j >= 1)
    pl.semaphore_wait(barrier, targets)

    def copy(go, src, dst, slot, di, dj, sem):
        rdma = pltpu.make_async_remote_copy(
            src_ref=src,
            dst_ref=dst,
            send_sem=send_sem.at[sem],
            recv_sem=recv_sem.at[slot],
            device_id=(di, dj),
            device_id_type=MESH,
        )
        rdma.start() if go else rdma.wait_send()

    def landing(half, slot):
        if slot < 2:
            return own.at[half, pl.ds(0, WIDE_ROWS)], wide.at[slot, i]
        return own.at[half], near.at[slot - 2, i]

    def push(go, di, dj, half, block, sem):
        for slot, low, high in places(block):

            @pl.when((di >= low) & (di <= high))
            def _(slot=slot):
                copy(go, *landing(half, slot), slot, di, dj, sem)

    def exchange(go):
        @pl.loop(0, N)
        def _(step):
            di = lax.rem(i + step, N)

            @pl.when(step > 0)
            def _():
                for half in range(2):
                    push(go, di, j, half, 2 + half, half * N + step)

            @pl.when(j <= N - 2)
            def _():
                for half in range(2):
                    push(go, di, j + 1, half, half, (2 + half) * N + step)

            @pl.when((di == 0) & (j <= N - 3))
            def _():
                copy(go, *landing(1, 0), 0, di, j + 2, 0)

            @pl.when((di == N - 1) & (j >= 1))
            def _():
                copy(go, *landing(0, 3), 3, di, j - 1, N)

    exchange(True)

    for half in range(2):
        for slot, low, high in places(2 + half):

            @pl.when((i >= low) & (i <= high))
            def _(half=half, slot=slot):
                pltpu.make_async_copy(*landing(half, slot), recv_sem.at[slot]).start()

    for q in range(4):

        @pl.when(slot_filled(q))
        def _(q=q):
            pltpu.make_async_copy(slots[q], slots[q], recv_sem.at[q]).wait()

    exchange(False)


def gather(own):
    return pl.pallas_call(
        gather_kernel,
        out_shape=(
            jax.ShapeDtypeStruct((2, N, WIDE_ROWS, LANES), jnp.bfloat16),
            jax.ShapeDtypeStruct((2, N, 2 * CH_ROWS, LANES), jnp.bfloat16),
        ),
        in_specs=[pl.BlockSpec(memory_space=pltpu.VMEM)],
        out_specs=(pl.BlockSpec(memory_space=pltpu.VMEM),) * 2,
        scratch_shapes=[
            pltpu.SemaphoreType.DMA((4 * N,)),
            pltpu.SemaphoreType.DMA((4,)),
        ],
        compiler_params=pltpu.CompilerParams(
            collective_id=0, has_side_effects=True, vmem_limit_bytes=32 * 2**20
        ),
        name="gather_features",
    )(own)


def dot(a, b, dims=(((1,), (0,)), ((), ()))):
    return lax.dot_general(a, b, dims, preferred_element_type=jnp.float32)


def iota(shape, dim):
    return lax.broadcasted_iota(jnp.int32, shape, dim)


def one_hot(mask):
    return jnp.where(mask, 1.0, 0.0).astype(jnp.bfloat16)


def spread_first(weights, out):
    rows, lane = iota((CH_ROWS, LANES), 0), iota((CH_ROWS, LANES), 1)
    r = lane % 16
    flat = weights[...].reshape(27 * F, CH_ROWS)
    parts = [
        dot(flat, one_hot((rows == lane // 16 * 5 + r // 2) & (r < 10) & (r % 2 == h))) for h in range(2)
    ]
    parts = [part.reshape(3, 3, 3, F, LANES) for part in parts]
    for a in range(3):
        for to in range(2):
            for ho in range(2):
                row = ((a * 2 + to) * 2 + ho) * F
                for ti in range(4):
                    e = ti - to
                    if 0 <= e < 3:
                        block = parts[0][a, 1 - ho, e] + parts[1][a, 2 - ho, e]
                    else:
                        block = jnp.zeros((F, LANES), jnp.float32)
                    out[row : row + F, ti * LANES : (ti + 1) * LANES] = block.astype(jnp.bfloat16)


def spread_later(weights, out):
    rows, lane = iota((F, LANES), 0), iota((F, LANES), 1)
    flat = weights[...].reshape(27 * F, F)
    parts = [dot(flat, one_hot(rows == lane - k * F)).reshape(3, 3, 3, F, LANES) for k in range(4)]
    for a in range(3):
        for to in range(2):
            for ho in range(2):
                row = ((a * 2 + to) * 2 + ho) * F
                for pair in range(2):
                    block = jnp.zeros((F, LANES), jnp.float32)
                    for k in range(4):
                        e, h = pair * 2 + k // 2 - to, k % 2
                        if 0 <= e < 3:
                            block = block + parts[k][a, 1 + h - ho, e]
                    out[row : row + F, pair * LANES : (pair + 1) * LANES] = block.astype(jnp.bfloat16)


def filter_pair(kernel, x):
    taps = dot(kernel, x)
    rows = 2 * 2 * F
    lane = iota((rows, DISP), 1)
    before = jnp.where(lane == DISP - 1, 0.0, pltpu.roll(taps[:rows], DISP - 1, 1))
    after = jnp.where(lane == 0, 0.0, pltpu.roll(taps[2 * rows :], 1, 1))
    return jnp.maximum(taps[rows : 2 * rows] + before + after, 0.0)


def filter_kernel(wide, near, w1, w2, w3, head, out, k1, k2, k3, right, x0, x1, x2, scores):
    i, j = lax.axis_index("disp"), lax.axis_index("col")
    spread_first(w1, k1)
    spread_later(w2, k2)
    spread_later(w3, k3)

    start = 16 * i - 2 - LANES * first_block(i)
    lane = iota((80, LANES), 1)
    r, lane80 = iota((16, 80), 0), iota((16, 80), 1)
    group_mask = jnp.where((lane80 // 16 == r // 2) & (lane80 % 2 == r % 2), 0.125, 0.0)
    pick = one_hot(iota((32, 2 * LANES), 1) == start - 1 + iota((32, 2 * LANES), 0))
    for s in range(8):
        pair = pl.ds(2 * s, 2)
        blocks = [ref[q, pair].astype(jnp.float32) for ref in (wide, near) for q in range(2)]
        turned = [
            pltpu.roll(block[:, :CH_ROWS].reshape(80, LANES), LANES - start, 1) for block in blocks
        ]
        for m in range(3):
            moved = jnp.where(lane < LANES - start, turned[m], turned[m + 1])
            right[s, :, m * LANES : (m + 1) * LANES] = moved.astype(jnp.bfloat16)
        left = [block[:, CH_ROWS:].reshape(80, LANES).astype(jnp.bfloat16) for block in blocks[2:]]
        picked = dot(pick[:, :LANES], left[0], NT) + dot(pick[:, LANES:], left[1], NT)
        spread = picked[:COLS0].reshape(COLS0, 1, 80) * group_mask[None]
        spread = spread.reshape(COLS0 * 16, 80).astype(jnp.bfloat16)
        products = dot(spread, right[s])
        for k in range(COLS0):
            strip = products[k * 16 : (k + 1) * 16]
            if k:
                strip = pltpu.roll(strip, 3 * LANES - k, 1)
            x0[k * LANES + s * 16 : k * LANES + s * 16 + 16] = strip[:, :DISP].astype(jnp.bfloat16)

    leftmost, rightmost = (i == 0) & (j == 0), (i == N - 1) & (j == N - 1)
    to = iota((LANES, DISP), 0) // 64
    for p in range(COLS1 // 2):
        y = filter_pair(k1[...], x0[p * 256 : p * 256 + 512])
        if p == 0:
            y = jnp.where(leftmost, 0.0, y)
        if p == COLS1 // 2 - 1:
            y = jnp.where(rightmost, 0.0, y)
        x1[p * LANES : (p + 1) * LANES] = y.astype(jnp.bfloat16)
    for p in range(COLS2 // 2):
        y = filter_pair(k2[...], x1[p * LANES : p * LANES + 256])
        if p == 0:
            y = jnp.where(leftmost & (to == 0), 0.0, y)
        if p == COLS2 // 2 - 1:
            y = jnp.where(rightmost & (to == 1), 0.0, y)
        x2[p * LANES : (p + 1) * LANES] = y.astype(jnp.bfloat16)
    for p in range(COLS3 // 2):
        y = filter_pair(k3[...], x2[p * LANES : p * LANES + 256])
        y = jnp.sum((y * head[...]).reshape(4, F, DISP), axis=1)
        for t in range(2):
            for h in range(2):
                row = h * 16 + 2 * p + t
                scores[row : row + 1] = y[2 * t + h : 2 * t + h + 1]

    disp = DISP - 1 - iota((32, DISP), 1)
    column = (N * j + i) * 16 + iota((32, DISP), 0) % 16
    valid = column >= disp
    score = jnp.where(valid, scores[...], MASKED)
    top = jnp.max(score, axis=1, keepdims=True)
    weighting = jnp.where(valid, jnp.exp(score - top), 0.0)
    denominator = jnp.sum(weighting, axis=1, keepdims=True)
    disparity = jnp.sum(weighting * disp.astype(jnp.float32), axis=1, keepdims=True) / denominator / DISP
    padded = jnp.concatenate([weighting, jnp.zeros((32, LANES), jnp.float32)], axis=1)
    band = jnp.concatenate(
        [pltpu.roll(padded[h * 16 : h * 16 + 16], 3, 1, stride=1, stride_axis=0) for h in range(2)], axis=0
    )
    high = band.astype(jnp.bfloat16)
    low = (band - high.astype(jnp.float32)).astype(jnp.bfloat16)
    band = jnp.concatenate([high, low], axis=0)
    out_lane = iota((16, LANES), 1)
    disp_high = disparity.astype(jnp.bfloat16).astype(jnp.float32)
    disp_low = disparity - disp_high
    tail = jnp.zeros((16, LANES), jnp.float32)
    for n, column_of in enumerate((disp_high[:16], disp_high[16:], disp_low[:16], disp_low[16:])):
        tail = jnp.where(out_lane == 80 + n, column_of, tail)
    even = iota((16, 80), 1) % 2 == 0
    for s in range(8):
        summed = dot(band, right[s], NT)
        warped = (summed[:32] + summed[32:]) / denominator
        picked = jnp.where(even, warped[:16], warped[16:])
        picked = jnp.concatenate([picked, jnp.zeros((16, LANES - 80), jnp.float32)], axis=1)
        out[s] = jnp.where(out_lane < 80, picked, tail).astype(jnp.bfloat16)


def filtered(wide, near, w1, w2, w3, head):
    vmem = pl.BlockSpec(memory_space=pltpu.VMEM)
    return pl.pallas_call(
        filter_kernel,
        out_shape=jax.ShapeDtypeStruct((8, 16, LANES), jnp.bfloat16),
        in_specs=[vmem] * 6,
        out_specs=vmem,
        scratch_shapes=[
            pltpu.VMEM((384, 512), jnp.bfloat16),
            pltpu.VMEM((384, 256), jnp.bfloat16),
            pltpu.VMEM((384, 256), jnp.bfloat16),
            pltpu.VMEM((8, 80, 384), jnp.bfloat16),
            pltpu.VMEM((COLS0 * 128, DISP), jnp.bfloat16),
            pltpu.VMEM((COLS1 * 64, DISP), jnp.bfloat16),
            pltpu.VMEM((COLS2 * 64, DISP), jnp.bfloat16),
            pltpu.VMEM((32, DISP), jnp.float32),
        ],
        compiler_params=pltpu.CompilerParams(vmem_limit_bytes=48 * 2**20),
        name="filter_columns",
    )(wide, near, w1, w2, w3, head)


def scatter_kernel(parts, warped, disparity, held, send_sem, recv_sem):
    i, j = lax.axis_index("disp"), lax.axis_index("col")
    barrier = pltpu.get_barrier_semaphore()

    @pl.loop(1, N)
    def _(step):
        pl.semaphore_signal(barrier, inc=1, device_id=(lax.rem(i + step, N), j), device_id_type=MESH)

    pl.semaphore_wait(barrier, N - 1)

    def push(step, go):
        di = lax.rem(i + step, N)
        rdma = pltpu.make_async_remote_copy(
            src_ref=parts.at[lax.div(di, 2)],
            dst_ref=held.at[i],
            send_sem=send_sem.at[step],
            recv_sem=recv_sem,
            device_id=(di, j),
            device_id_type=MESH,
        )
        rdma.start() if go else rdma.wait_send()

    pl.loop(1, N)(lambda step: push(step, True))
    pltpu.make_async_copy(parts.at[lax.div(i, 2)], held.at[i], recv_sem).start()
    pltpu.make_async_copy(held, held, recv_sem).wait()
    pl.loop(1, N)(lambda step: push(step, False))
    rows, lane = iota((48, LANES), 0), iota((48, LANES), 1)
    mine = lane == lax.rem(i, 2) * CH_ROWS + rows
    tail = (lane == 40 + rows) | (lane == 42 + rows)
    pick = one_hot((mine & (rows < CH_ROWS)) | (tail & (rows >= CH_ROWS) & (rows < CH_ROWS + 2)))
    result = dot(pick, held[...].reshape(256, LANES), NT)
    warped[...] = result[:CH_ROWS].astype(jnp.bfloat16)
    disparity[...] = result[CH_ROWS : CH_ROWS + 2]


def scattered(parts):
    vmem = pl.BlockSpec(memory_space=pltpu.VMEM)
    return pl.pallas_call(
        scatter_kernel,
        out_shape=(
            jax.ShapeDtypeStruct((CH_ROWS, 256), jnp.bfloat16),
            jax.ShapeDtypeStruct((2, 256), jnp.float32),
        ),
        in_specs=[vmem],
        out_specs=(vmem, vmem),
        scratch_shapes=[
            pltpu.VMEM((N, 16, LANES), jnp.bfloat16),
            pltpu.SemaphoreType.DMA((N,)),
            pltpu.SemaphoreType.DMA,
        ],
        compiler_params=pltpu.CompilerParams(collective_id=1, has_side_effects=True),
        name="scatter_results",
    )(parts)


def shards(left_feat, right_feat, conv1_w, conv2_w, conv3_w, head_w):
    own = jnp.concatenate([right_feat.reshape(CH_ROWS, 2, LANES), left_feat.reshape(CH_ROWS, 2, LANES)])
    own = jnp.transpose(own, (1, 0, 2))
    w1, w2, w3 = (jnp.transpose(w, (2, 3, 4, 0, 1)) for w in (conv1_w, conv2_w, conv3_w))
    head = jnp.tile(head_w, 4).reshape(128, 1)
    wide, near = gather(own)
    parts = filtered(wide, near, w1, w2, w3, head)
    warped, disparity = scattered(parts)
    return warped.reshape(20, 2, 256), disparity


def solution(mesh):
    return jax.shard_map(
        shards,
        mesh=mesh,
        in_specs=(P("disp", None, "col"), P("disp", None, "col"), P(), P(), P(), P()),
        out_specs=(P("disp", None, "col"), P(None, "col")),
        check_vma=False,
    )
```

```python
import jax
import jax.numpy as jnp
from jax import lax
from jax.experimental import pallas as pl
from jax.experimental.pallas import tpu as pltpu
from jax.sharding import PartitionSpec as P

N = 16
LANES = 128
DISP = 256
CH_ROWS = 40
WIDE_ROWS = 48
COLS0, COLS1, COLS2, COLS3 = 22, 20, 18, 16
F = 32
MASKED = -1e30
MESH = pl.DeviceIdType.MESH
NT = (((1,), (1,)), ((), ()))


def first_block(i):
    return lax.div(i + 7, 8) - 1


def places(block):
    for low, high, first in ((0, 0, -1), (1, 8, 0), (9, 15, 1)):
        slot = block - first
        if 0 <= slot < 4:
            yield slot, max(low, 7) if slot == 3 and high == 8 else low, high


def dot(a, b, dims=(((1,), (0,)), ((), ()))):
    return lax.dot_general(a, b, dims, preferred_element_type=jnp.float32)


def iota(shape, dim):
    return lax.broadcasted_iota(jnp.int32, shape, dim)


def one_hot(mask):
    return jnp.where(mask, 1.0, 0.0).astype(jnp.bfloat16)


def spread_first(weights, out):
    rows, lane = iota((CH_ROWS, LANES), 0), iota((CH_ROWS, LANES), 1)
    r = lane % 16
    flat = weights[...].reshape(27 * F, CH_ROWS)
    parts = [
        dot(flat, one_hot((rows == lane // 16 * 5 + r // 2) & (r < 10) & (r % 2 == h))) for h in range(2)
    ]
    parts = [part.reshape(3, 3, 3, F, LANES) for part in parts]
    for a in range(3):
        for to in range(2):
            for ho in range(2):
                row = ((a * 2 + to) * 2 + ho) * F
                for ti in range(4):
                    e = ti - to
                    if 0 <= e < 3:
                        block = parts[0][a, 1 - ho, e] + parts[1][a, 2 - ho, e]
                    else:
                        block = jnp.zeros((F, LANES), jnp.float32)
                    out[row : row + F, ti * LANES : (ti + 1) * LANES] = block.astype(jnp.bfloat16)


def spread_later(weights, out):
    rows, lane = iota((F, LANES), 0), iota((F, LANES), 1)
    flat = weights[...].reshape(27 * F, F)
    parts = [dot(flat, one_hot(rows == lane - k * F)).reshape(3, 3, 3, F, LANES) for k in range(4)]
    for a in range(3):
        for to in range(2):
            for ho in range(2):
                row = ((a * 2 + to) * 2 + ho) * F
                for pair in range(2):
                    block = jnp.zeros((F, LANES), jnp.float32)
                    for k in range(4):
                        e, h = pair * 2 + k // 2 - to, k % 2
                        if 0 <= e < 3:
                            block = block + parts[k][a, 1 + h - ho, e]
                    out[row : row + F, pair * LANES : (pair + 1) * LANES] = block.astype(jnp.bfloat16)


def filter_pair(kernel, x):
    taps = dot(kernel, x)
    rows = 2 * 2 * F
    lane = iota((rows, DISP), 1)
    before = jnp.where(lane == DISP - 1, 0.0, pltpu.roll(taps[:rows], DISP - 1, 1))
    after = jnp.where(lane == 0, 0.0, pltpu.roll(taps[2 * rows :], 1, 1))
    return jnp.maximum(taps[rows : 2 * rows] + before + after, 0.0)


def stereo_kernel(
    left_feat, right_feat, w1_hbm, w2_hbm, w3_hbm, head, warped, disparity_out,
    own, wide, near, parts, held, w1, w2, w3, k1, k2, k3, right, x0, x1, x2, scores,
    weight_sem, send_sem, recv_sem, result_send, result_recv,
):
    i, j = lax.axis_index("disp"), lax.axis_index("col")
    weights = ((w1_hbm, w1), (w2_hbm, w2), (w3_hbm, w3))
    for n, (src, dst) in enumerate(weights):
        pltpu.make_async_copy(src, dst, weight_sem.at[n]).start()
    for n, feat in enumerate((right_feat, left_feat)):
        flat = feat[...].astype(jnp.float32).reshape(CH_ROWS, 256).astype(jnp.bfloat16)
        for half in range(2):
            own[half, n * CH_ROWS : (n + 1) * CH_ROWS] = flat[:, half * LANES : (half + 1) * LANES]

    base = first_block(i)

    def slot_filled(q):
        block = 2 * (j - 1) + base + q
        filled = (block >= 0) & (block < 2 * N)
        if q == 3:
            filled = filled & ((lax.rem(i, 8) == 0) | (lax.rem(i, 8) == 7))
        return filled

    slots = [wide.at[0], wide.at[1], near.at[0], near.at[1]]
    for q in range(4):

        @pl.when(jnp.logical_not(slot_filled(q)))
        def _(q=q):
            slots[q][...] = jnp.zeros(slots[q].shape, jnp.bfloat16)

    barrier = pltpu.get_barrier_semaphore()

    def greet(di, dj):
        pl.semaphore_signal(barrier, inc=1, device_id=(di, dj), device_id_type=MESH)

    def greet_strip(dj):
        @pl.loop(0, N)
        def _(step):
            greet(lax.rem(i + step, N), dj)

    @pl.loop(1, N)
    def _(step):
        greet(lax.rem(i + step, N), j)

    pl.when(j >= 1)(lambda: greet_strip(j - 1))
    pl.when((i == 0) & (j >= 2))(lambda: greet_strip(j - 2))
    pl.when((i == N - 1) & (j <= N - 2))(lambda: greet_strip(j + 1))
    targets = N - 1 + N * (j <= N - 2) + (j <= N - 3) + (j >= 1)
    pl.semaphore_wait(barrier, targets)

    def copy(go, src, dst, slot, di, dj, sem):
        rdma = pltpu.make_async_remote_copy(
            src_ref=src,
            dst_ref=dst,
            send_sem=send_sem.at[sem],
            recv_sem=recv_sem.at[slot, lax.div(i, 2)],
            device_id=(di, dj),
            device_id_type=MESH,
        )
        rdma.start() if go else rdma.wait_send()

    def landing(half, slot):
        if slot < 2:
            return own.at[half, pl.ds(0, WIDE_ROWS)], wide.at[slot, i]
        return own.at[half], near.at[slot - 2, i]

    def push(go, di, dj, half, block, sem):
        for slot, low, high in places(block):

            @pl.when((di >= low) & (di <= high))
            def _(slot=slot):
                copy(go, *landing(half, slot), slot, di, dj, sem)

    def exchange(go):
        @pl.loop(0, N)
        def _(step):
            di = lax.rem(i + step, N)

            @pl.when(step > 0)
            def _():
                for half in range(2):
                    push(go, di, j, half, 2 + half, half * N + step)

            @pl.when(j <= N - 2)
            def _():
                for half in range(2):
                    push(go, di, j + 1, half, half, (2 + half) * N + step)

            @pl.when((di == 0) & (j <= N - 3))
            def _():
                copy(go, *landing(1, 0), 0, di, j + 2, 0)

            @pl.when((di == N - 1) & (j >= 1))
            def _():
                copy(go, *landing(0, 3), 3, di, j - 1, N)

    exchange(True)

    for half in range(2):
        for slot, low, high in places(2 + half):

            @pl.when((i >= low) & (i <= high))
            def _(half=half, slot=slot):
                pltpu.make_async_copy(*landing(half, slot), recv_sem.at[slot, lax.div(i, 2)]).start()

    for n, (src, dst) in enumerate(weights):
        pltpu.make_async_copy(src, dst, weight_sem.at[n]).wait()
    spread_first(w1, k1)
    spread_later(w2, k2)
    spread_later(w3, k3)

    start = 16 * i - 2 - LANES * base
    lane = iota((80, LANES), 1)
    r, lane80 = iota((16, 80), 0), iota((16, 80), 1)
    group_mask = jnp.where((lane80 // 16 == r // 2) & (lane80 % 2 == r % 2), 0.125, 0.0)
    pick = one_hot(iota((32, 2 * LANES), 1) == start - 1 + iota((32, 2 * LANES), 0))

    @pl.loop(0, 8)
    def _(n):
        s = lax.rem(lax.div(i, 2) + 8 - n, 8)
        pair = pl.ds(2 * s, 2)
        for q in range(4):

            @pl.when(slot_filled(q))
            def _(q=q):
                landed = slots[q].at[pair]
                pltpu.make_async_copy(landed, landed, recv_sem.at[q, s]).wait()

        blocks = [ref[q, pair].astype(jnp.float32) for ref in (wide, near) for q in range(2)]
        turned = [
            pltpu.roll(block[:, :CH_ROWS].reshape(80, LANES), LANES - start, 1) for block in blocks
        ]
        moved = [jnp.where(lane < LANES - start, turned[m], turned[m + 1]) for m in range(3)]
        moved = jnp.concatenate(moved, axis=1).astype(jnp.bfloat16)
        right[s] = moved
        left = [block[:, CH_ROWS:].reshape(80, LANES).astype(jnp.bfloat16) for block in blocks[2:]]
        picked = dot(pick[:, :LANES], left[0], NT) + dot(pick[:, LANES:], left[1], NT)
        spread = picked[:COLS0].reshape(COLS0, 1, 80) * group_mask[None]
        spread = spread.reshape(COLS0 * 16, 80).astype(jnp.bfloat16)
        products = dot(spread, moved)
        for k in range(COLS0):
            strip = products[k * 16 : (k + 1) * 16]
            if k:
                strip = pltpu.roll(strip, 3 * LANES - k, 1)
            place = pl.ds(pl.multiple_of(k * LANES + s * 16, 16), 16)
            x0[place] = strip[:, :DISP].astype(jnp.bfloat16)

    exchange(False)

    leftmost, rightmost = (i == 0) & (j == 0), (i == N - 1) & (j == N - 1)
    to = iota((LANES, DISP), 0) // 64
    for p in range(COLS1 // 2):
        y = filter_pair(k1[...], x0[p * 256 : p * 256 + 512])
        if p == 0:
            y = jnp.where(leftmost, 0.0, y)
        if p == COLS1 // 2 - 1:
            y = jnp.where(rightmost, 0.0, y)
        x1[p * LANES : (p + 1) * LANES] = y.astype(jnp.bfloat16)
    for p in range(COLS2 // 2):
        y = filter_pair(k2[...], x1[p * LANES : p * LANES + 256])
        if p == 0:
            y = jnp.where(leftmost & (to == 0), 0.0, y)
        if p == COLS2 // 2 - 1:
            y = jnp.where(rightmost & (to == 1), 0.0, y)
        x2[p * LANES : (p + 1) * LANES] = y.astype(jnp.bfloat16)
    for p in range(COLS3 // 2):
        y = filter_pair(k3[...], x2[p * LANES : p * LANES + 256])
        y = jnp.sum((y * head[...]).reshape(4, F, DISP), axis=1)
        for t in range(2):
            for h in range(2):
                row = h * 16 + 2 * p + t
                scores[row : row + 1] = y[2 * t + h : 2 * t + h + 1]

    disp = DISP - 1 - iota((32, DISP), 1)
    column = (N * j + i) * 16 + iota((32, DISP), 0) % 16
    valid = column >= disp
    score = jnp.where(valid, scores[...], MASKED)
    top = jnp.max(score, axis=1, keepdims=True)
    weighting = jnp.where(valid, jnp.exp(score - top), 0.0)
    denominator = jnp.sum(weighting, axis=1, keepdims=True)
    disparity = jnp.sum(weighting * disp.astype(jnp.float32), axis=1, keepdims=True) / denominator / DISP
    padded = jnp.concatenate([weighting, jnp.zeros((32, LANES), jnp.float32)], axis=1)
    band = jnp.concatenate(
        [pltpu.roll(padded[h * 16 : h * 16 + 16], 3, 1, stride=1, stride_axis=0) for h in range(2)], axis=0
    )
    high = band.astype(jnp.bfloat16)
    low = (band - high.astype(jnp.float32)).astype(jnp.bfloat16)
    band = jnp.concatenate([high, low], axis=0)
    out_lane = iota((16, LANES), 1)
    disp_high = disparity.astype(jnp.bfloat16).astype(jnp.float32)
    disp_low = disparity - disp_high
    tail = jnp.zeros((16, LANES), jnp.float32)
    for n, column_of in enumerate((disp_high[:16], disp_high[16:], disp_low[:16], disp_low[16:])):
        tail = jnp.where(out_lane == 80 + n, column_of, tail)
    even = iota((16, 80), 1) % 2 == 0

    def push_result(di, s, go):
        rdma = pltpu.make_async_remote_copy(
            src_ref=parts.at[s],
            dst_ref=held.at[i],
            send_sem=result_send.at[di],
            recv_sem=result_recv,
            device_id=(di, j),
            device_id_type=MESH,
        )
        rdma.start() if go else rdma.wait_send()

    def each_result(s, go):
        for core in range(2):
            di = 2 * s + core
            pl.when(di != i)(lambda di=di: push_result(di, s, go))

    @pl.loop(0, 8)
    def _(n):
        s = lax.rem(lax.div(i, 2) + 1 + n, 8)
        summed = dot(band, right[s], NT)
        mean = (summed[:32] + summed[32:]) / denominator
        picked = jnp.where(even, mean[:16], mean[16:])
        picked = jnp.concatenate([picked, jnp.zeros((16, LANES - 80), jnp.float32)], axis=1)
        parts[s] = jnp.where(out_lane < 80, picked, tail).astype(jnp.bfloat16)
        each_result(s, True)

    pltpu.make_async_copy(parts.at[lax.div(i, 2)], held.at[i], result_recv).start()
    pltpu.make_async_copy(held, held, result_recv).wait()
    pl.loop(0, 8)(lambda s: each_result(s, False))
    rows, lane = iota((48, LANES), 0), iota((48, LANES), 1)
    mine = lane == lax.rem(i, 2) * CH_ROWS + rows
    extra = (lane == 40 + rows) | (lane == 42 + rows)
    pick = one_hot((mine & (rows < CH_ROWS)) | (extra & (rows >= CH_ROWS) & (rows < CH_ROWS + 2)))
    result = dot(pick, held[...].reshape(256, LANES), NT)
    warped[...] = result[:CH_ROWS].reshape(20, 2, 256).astype(jnp.bfloat16)
    disparity_out[...] = result[CH_ROWS : CH_ROWS + 2]


def shards(left_feat, right_feat, conv1_w, conv2_w, conv3_w, head_w):
    w1, w2, w3 = (jnp.transpose(w, (2, 3, 4, 0, 1)) for w in (conv1_w, conv2_w, conv3_w))
    head = jnp.tile(head_w, 4).reshape(128, 1)
    vmem, anywhere = pl.BlockSpec(memory_space=pltpu.VMEM), pl.BlockSpec(memory_space=pl.ANY)
    bf16, dma = jnp.bfloat16, pltpu.SemaphoreType.DMA
    return pl.pallas_call(
        stereo_kernel,
        out_shape=(
            jax.ShapeDtypeStruct((20, 2, 256), bf16),
            jax.ShapeDtypeStruct((2, 256), jnp.float32),
        ),
        in_specs=[vmem, vmem, anywhere, anywhere, anywhere, vmem],
        out_specs=(vmem, vmem),
        scratch_shapes=[
            pltpu.VMEM((2, 2 * CH_ROWS, LANES), bf16),
            pltpu.VMEM((2, N, WIDE_ROWS, LANES), bf16),
            pltpu.VMEM((2, N, 2 * CH_ROWS, LANES), bf16),
            pltpu.VMEM((8, 16, LANES), bf16),
            pltpu.VMEM((N, 16, LANES), bf16),
            pltpu.VMEM(w1.shape, bf16),
            pltpu.VMEM(w2.shape, bf16),
            pltpu.VMEM(w3.shape, bf16),
            pltpu.VMEM((384, 512), bf16),
            pltpu.VMEM((384, 256), bf16),
            pltpu.VMEM((384, 256), bf16),
            pltpu.VMEM((8, 80, 384), bf16),
            pltpu.VMEM((COLS0 * 128, DISP), bf16),
            pltpu.VMEM((COLS1 * 64, DISP), bf16),
            pltpu.VMEM((COLS2 * 64, DISP), bf16),
            pltpu.VMEM((32, DISP), jnp.float32),
            dma((3,)),
            dma((4 * N,)),
            dma((4, 8)),
            dma((N,)),
            dma,
        ],
        compiler_params=pltpu.CompilerParams(
            collective_id=0, has_side_effects=True, vmem_limit_bytes=56 * 2**20
        ),
        name="stereo",
    )(left_feat, right_feat, w1, w2, w3, head)


def solution(mesh):
    return jax.shard_map(
        shards,
        mesh=mesh,
        in_specs=(P("disp", None, "col"), P("disp", None, "col"), P(), P(), P(), P()),
        out_specs=(P("disp", None, "col"), P(None, "col")),
        check_vma=False,
    )
```

```python
import jax
import jax.numpy as jnp
from jax import lax
from jax.experimental import pallas as pl
from jax.experimental.pallas import tpu as pltpu
from jax.sharding import PartitionSpec as P

N = 16
LANES = 128
DISP = 256
CH_ROWS = 40
SLOT_ROWS = (48, 48, 80, 80)
SLOT_START = (0, 48, 96, 176)
BASE_SHIFT = 14
COLS0, COLS1, COLS2, COLS3 = 22, 20, 18, 16
F = 32
MASKED = -1e30
MESH = pl.DeviceIdType.MESH
NT = (((1,), (1,)), ((), ()))


def first_block(chip):
    return lax.div(chip + 3, 4) - 1


def places(block):
    for low, high, first in ((0, 0, -1), (1, 4, 0), (5, 7, 1)):
        slot = block - first
        if 0 <= slot < 4:
            yield slot, max(low, 3) if slot == 3 and high == 4 else low, high


def dot(a, b, dims=(((1,), (0,)), ((), ()))):
    return lax.dot_general(a, b, dims, preferred_element_type=jnp.float32)


def iota(shape, dim):
    return lax.broadcasted_iota(jnp.int32, shape, dim)


def one_hot(mask):
    return jnp.where(mask, 1.0, 0.0).astype(jnp.bfloat16)


def spread_first(weights, out):
    rows, lane = iota((CH_ROWS, LANES), 0), iota((CH_ROWS, LANES), 1)
    r = lane % 16
    flat = weights[...].reshape(27 * F, CH_ROWS)
    parts = [
        dot(flat, one_hot((rows == lane // 16 * 5 + r // 2) & (r < 10) & (r % 2 == h))) for h in range(2)
    ]
    parts = [part.reshape(3, 3, 3, F, LANES) for part in parts]
    for a in range(3):
        for to in range(2):
            for ho in range(2):
                row = ((a * 2 + to) * 2 + ho) * F
                for ti in range(4):
                    e = ti - to
                    if 0 <= e < 3:
                        block = parts[0][a, 1 - ho, e] + parts[1][a, 2 - ho, e]
                    else:
                        block = jnp.zeros((F, LANES), jnp.float32)
                    out[row : row + F, ti * LANES : (ti + 1) * LANES] = block.astype(jnp.bfloat16)


def spread_later(weights, out):
    rows, lane = iota((F, LANES), 0), iota((F, LANES), 1)
    flat = weights[...].reshape(27 * F, F)
    parts = [dot(flat, one_hot(rows == lane - k * F)).reshape(3, 3, 3, F, LANES) for k in range(4)]
    for a in range(3):
        for to in range(2):
            for ho in range(2):
                row = ((a * 2 + to) * 2 + ho) * F
                for pair in range(2):
                    block = jnp.zeros((F, LANES), jnp.float32)
                    for k in range(4):
                        e, h = pair * 2 + k // 2 - to, k % 2
                        if 0 <= e < 3:
                            block = block + parts[k][a, 1 + h - ho, e]
                    out[row : row + F, pair * LANES : (pair + 1) * LANES] = block.astype(jnp.bfloat16)


def filter_pair(kernel, x):
    taps = dot(kernel, x)
    rows = 2 * 2 * F
    lane = iota((rows, DISP), 1)
    before = jnp.where(lane == DISP - 1, 0.0, pltpu.roll(taps[:rows], DISP - 1, 1))
    after = jnp.where(lane == 0, 0.0, pltpu.roll(taps[2 * rows :], 1, 1))
    return jnp.maximum(taps[rows : 2 * rows] + before + after, 0.0)


def stereo_kernel(
    left_feat, right_feat, w1_hbm, w2_hbm, w3_hbm, head, warped, disparity_out,
    own, land, parts, held, w1, w2, w3, k1, k2, k3, right, x0, x1, x2, scores,
    weight_sem, send_sem, recv_sem, pass_send, pass_recv, result_send, result_recv,
):
    i, j = lax.axis_index("disp"), lax.axis_index("col")
    chip, core = lax.div(i, 2), lax.rem(i, 2)
    base = first_block(chip)
    weights = ((w1_hbm, w1), (w2_hbm, w2), (w3_hbm, w3))
    for n, (src, dst) in enumerate(weights):
        pltpu.make_async_copy(src, dst, weight_sem.at[n]).start()
    for n, feat in enumerate((right_feat, left_feat)):
        flat = feat[...].astype(jnp.float32).reshape(CH_ROWS, 256).astype(jnp.bfloat16)
        for half in range(2):
            own[half, n * CH_ROWS : (n + 1) * CH_ROWS] = flat[:, half * LANES : (half + 1) * LANES]

    def slot_filled(slot):
        block = 2 * (j - 1) + base + slot
        filled = (block >= 0) & (block < 2 * N)
        if slot == 3:
            filled = filled & ((lax.rem(chip, 4) == 0) | (lax.rem(chip, 4) == 3))
        return filled

    def slot_rows(slot):
        return pl.ds(SLOT_START[slot], SLOT_ROWS[slot])

    for slot in range(4):

        @pl.when(jnp.logical_not(slot_filled(slot)))
        def _(slot=slot):
            for n in range(8):
                land[2 * n + core, slot_rows(slot)] = jnp.zeros((SLOT_ROWS[slot], LANES), jnp.bfloat16)

    barrier = pltpu.get_barrier_semaphore()

    def greet(di, dj):
        pl.semaphore_signal(barrier, inc=1, device_id=(di, dj), device_id_type=MESH)

    def greet_strip(dj):
        @pl.loop(0, 8)
        def _(step):
            greet(2 * lax.rem(chip + step, 8) + core, dj)

    @pl.loop(1, N)
    def _(step):
        greet(lax.rem(i + step, N), j)

    pl.when(j >= 1)(lambda: greet_strip(j - 1))
    pl.when((chip == 0) & (j >= 2))(lambda: greet_strip(j - 2))
    pl.when((chip == 7) & (j <= N - 2))(lambda: greet_strip(j + 1))
    targets = N - 1 + 8 * (j <= N - 2) + (j <= N - 3) + (j >= 1)
    pl.semaphore_wait(barrier, targets)

    def landing(half, slot):
        return own.at[half, pl.ds(0, SLOT_ROWS[slot])], land.at[i, slot_rows(slot)]

    def copy(go, half, slot, to_chip, dj, sem):
        src, dst = landing(half, slot)
        rdma = pltpu.make_async_remote_copy(
            src_ref=src,
            dst_ref=dst,
            send_sem=send_sem.at[sem],
            recv_sem=recv_sem.at[slot, chip],
            device_id=(2 * to_chip + core, dj),
            device_id_type=MESH,
        )
        rdma.start() if go else rdma.wait_send()

    def push(go, to_chip, dj, half, block, sem):
        for slot, low, high in places(block):

            @pl.when((to_chip >= low) & (to_chip <= high))
            def _(slot=slot):
                copy(go, half, slot, to_chip, dj, sem)

    def exchange(go):
        @pl.loop(0, 8)
        def _(step):
            to_chip = lax.rem(chip + step, 8)

            @pl.when(step > 0)
            def _():
                for half in range(2):
                    push(go, to_chip, j, half, 2 + half, half * 8 + step)

            @pl.when(j <= N - 2)
            def _():
                for half in range(2):
                    push(go, to_chip, j + 1, half, half, (2 + half) * 8 + step)

            @pl.when((to_chip == 0) & (j <= N - 3))
            def _():
                copy(go, 1, 0, to_chip, j + 2, 0)

            @pl.when((to_chip == 7) & (j >= 1))
            def _():
                copy(go, 0, 3, to_chip, j - 1, 8)

    exchange(True)

    for half in range(2):
        for slot, low, high in places(2 + half):

            @pl.when((chip >= low) & (chip <= high))
            def _(half=half, slot=slot):
                pltpu.make_async_copy(*landing(half, slot), recv_sem.at[slot, chip]).start()

    for n, (src, dst) in enumerate(weights):
        pltpu.make_async_copy(src, dst, weight_sem.at[n]).wait()
    spread_first(w1, k1)
    spread_later(w2, k2)
    spread_later(w3, k3)

    start = 16 * i - 2 - BASE_SHIFT - LANES * base
    lane = iota((80, LANES), 1)
    r, lane80 = iota((16, 80), 0), iota((16, 80), 1)
    group_mask = jnp.where((lane80 // 16 == r // 2) & (lane80 % 2 == r % 2), 0.125, 0.0)
    pick = one_hot(iota((32, 2 * LANES), 1) == start + BASE_SHIFT - 1 + iota((32, 2 * LANES), 0))

    def pass_on(s, go):
        held_here = land.at[2 * s + core]
        rdma = pltpu.make_async_remote_copy(
            src_ref=held_here,
            dst_ref=held_here,
            send_sem=pass_send.at[s],
            recv_sem=pass_recv.at[s],
            device_id=(2 * chip + 1 - core, j),
            device_id_type=MESH,
        )
        rdma.start() if go else rdma.wait_send()

    def arrive(n):
        s = lax.rem(chip + 8 - n, 8)
        for slot in range(4):

            @pl.when(slot_filled(slot))
            def _(slot=slot):
                landed = land.at[2 * s + core, slot_rows(slot)]
                pltpu.make_async_copy(landed, landed, recv_sem.at[slot, s]).wait()

        pass_on(s, True)

    arrive(0)

    @pl.loop(0, 8)
    def _(n):
        pl.when(n < 7)(lambda: arrive(n + 1))
        s = lax.rem(chip + 8 - n, 8)
        pair = pl.ds(2 * s, 2)
        passed = land.at[2 * s + 1 - core]
        pltpu.make_async_copy(passed, passed, pass_recv.at[s]).wait()
        blocks = [land[pair, slot_rows(slot)].astype(jnp.float32) for slot in range(4)]
        turned = [
            pltpu.roll(block[:, :CH_ROWS].reshape(80, LANES), LANES - start, 1) for block in blocks
        ]
        moved = [jnp.where(lane < LANES - start, turned[m], turned[m + 1]) for m in range(3)]
        moved = jnp.concatenate(moved, axis=1).astype(jnp.bfloat16)
        right[s] = moved
        left = [block[:, CH_ROWS:].reshape(80, LANES).astype(jnp.bfloat16) for block in blocks[2:]]
        picked = dot(pick[:, :LANES], left[0], NT) + dot(pick[:, LANES:], left[1], NT)
        spread = picked[:COLS0].reshape(COLS0, 1, 80) * group_mask[None]
        spread = spread.reshape(COLS0 * 16, 80).astype(jnp.bfloat16)
        products = dot(spread, moved)
        for k in range(COLS0):
            strip = products[k * 16 : (k + 1) * 16]
            strip = pltpu.roll(strip, 3 * LANES - BASE_SHIFT - k, 1)
            place = pl.ds(pl.multiple_of(k * LANES + s * 16, 16), 16)
            x0[place] = strip[:, :DISP].astype(jnp.bfloat16)

    exchange(False)
    pl.loop(0, 8)(lambda s: pass_on(s, False))
    head_rows = jnp.where(iota((LANES, F), 0) % F == iota((LANES, F), 1), head[...], 0.0)
    head_column = jnp.sum(head_rows, axis=1, keepdims=True)

    leftmost, rightmost = (i == 0) & (j == 0), (i == N - 1) & (j == N - 1)
    to = iota((LANES, DISP), 0) // 64
    for p in range(COLS1 // 2):
        y = filter_pair(k1[...], x0[p * 256 : p * 256 + 512])
        if p == 0:
            y = jnp.where(leftmost, 0.0, y)
        if p == COLS1 // 2 - 1:
            y = jnp.where(rightmost, 0.0, y)
        x1[p * LANES : (p + 1) * LANES] = y.astype(jnp.bfloat16)
    for p in range(COLS2 // 2):
        y = filter_pair(k2[...], x1[p * LANES : p * LANES + 256])
        if p == 0:
            y = jnp.where(leftmost & (to == 0), 0.0, y)
        if p == COLS2 // 2 - 1:
            y = jnp.where(rightmost & (to == 1), 0.0, y)
        x2[p * LANES : (p + 1) * LANES] = y.astype(jnp.bfloat16)
    for p in range(COLS3 // 2):
        y = filter_pair(k3[...], x2[p * LANES : p * LANES + 256])
        y = jnp.sum((y * head_column).reshape(4, F, DISP), axis=1)
        for t in range(2):
            for h in range(2):
                row = h * 16 + 2 * p + t
                scores[row : row + 1] = y[2 * t + h : 2 * t + h + 1]

    disp = DISP - 1 - iota((32, DISP), 1)
    column = (N * j + i) * 16 + iota((32, DISP), 0) % 16
    valid = column >= disp
    score = jnp.where(valid, scores[...], MASKED)
    top = jnp.max(score, axis=1, keepdims=True)
    weighting = jnp.where(valid, jnp.exp(score - top), 0.0)
    denominator = jnp.sum(weighting, axis=1, keepdims=True)
    disparity = jnp.sum(weighting * disp.astype(jnp.float32), axis=1, keepdims=True) / denominator / DISP
    padded = jnp.concatenate([weighting, jnp.zeros((32, LANES), jnp.float32)], axis=1)
    band = jnp.concatenate(
        [pltpu.roll(padded[h * 16 : h * 16 + 16], BASE_SHIFT + 3, 1, stride=1, stride_axis=0) for h in range(2)], axis=0
    )
    high = band.astype(jnp.bfloat16)
    low = (band - high.astype(jnp.float32)).astype(jnp.bfloat16)
    band = jnp.concatenate([high, low], axis=0)
    out_lane = iota((16, LANES), 1)
    disp_high = disparity.astype(jnp.bfloat16).astype(jnp.float32)
    disp_low = disparity - disp_high
    tail = jnp.zeros((16, LANES), jnp.float32)
    for n, column_of in enumerate((disp_high[:16], disp_high[16:], disp_low[:16], disp_low[16:])):
        tail = jnp.where(out_lane == 80 + n, column_of, tail)
    even = iota((16, 80), 1) % 2 == 0

    def push_result(di, s, go):
        rdma = pltpu.make_async_remote_copy(
            src_ref=parts.at[s],
            dst_ref=held.at[i],
            send_sem=result_send.at[di],
            recv_sem=result_recv,
            device_id=(di, j),
            device_id_type=MESH,
        )
        rdma.start() if go else rdma.wait_send()

    def each_result(s, go):
        for core in range(2):
            di = 2 * s + core
            pl.when(di != i)(lambda di=di: push_result(di, s, go))

    @pl.loop(0, 8)
    def _(n):
        s = lax.rem(chip + 1 + n, 8)
        summed = dot(band, right[s], NT)
        mean = (summed[:32] + summed[32:]) / denominator
        picked = jnp.where(even, mean[:16], mean[16:])
        picked = jnp.concatenate([picked, jnp.zeros((16, LANES - 80), jnp.float32)], axis=1)
        parts[s] = jnp.where(out_lane < 80, picked, tail).astype(jnp.bfloat16)
        each_result(s, True)

    pltpu.make_async_copy(parts.at[chip], held.at[i], result_recv).start()
    pltpu.make_async_copy(held, held, result_recv).wait()
    pl.loop(0, 8)(lambda s: each_result(s, False))
    rows, lane = iota((48, LANES), 0), iota((48, LANES), 1)
    mine = lane == lax.rem(i, 2) * CH_ROWS + rows
    extra = (lane == 40 + rows) | (lane == 42 + rows)
    pick = one_hot((mine & (rows < CH_ROWS)) | (extra & (rows >= CH_ROWS) & (rows < CH_ROWS + 2)))
    result = dot(pick, held[...].reshape(256, LANES), NT)
    warped[...] = result[:CH_ROWS].reshape(20, 2, 256).astype(jnp.bfloat16)
    disparity_out[...] = result[CH_ROWS : CH_ROWS + 2]


def shards(left_feat, right_feat, conv1_w, conv2_w, conv3_w, head_w):
    w1, w2, w3 = (jnp.transpose(w, (2, 3, 4, 0, 1)) for w in (conv1_w, conv2_w, conv3_w))
    head = head_w.reshape(1, F)
    vmem, anywhere = pl.BlockSpec(memory_space=pltpu.VMEM), pl.BlockSpec(memory_space=pl.ANY)
    bf16, dma = jnp.bfloat16, pltpu.SemaphoreType.DMA
    return pl.pallas_call(
        stereo_kernel,
        out_shape=(
            jax.ShapeDtypeStruct((20, 2, 256), bf16),
            jax.ShapeDtypeStruct((2, 256), jnp.float32),
        ),
        in_specs=[vmem, vmem, anywhere, anywhere, anywhere, vmem],
        out_specs=(vmem, vmem),
        scratch_shapes=[
            pltpu.VMEM((2, 2 * CH_ROWS, LANES), bf16),
            pltpu.VMEM((N, 256, LANES), bf16),
            pltpu.VMEM((8, 16, LANES), bf16),
            pltpu.VMEM((N, 16, LANES), bf16),
            pltpu.VMEM(w1.shape, bf16),
            pltpu.VMEM(w2.shape, bf16),
            pltpu.VMEM(w3.shape, bf16),
            pltpu.VMEM((384, 512), bf16),
            pltpu.VMEM((384, 256), bf16),
            pltpu.VMEM((384, 256), bf16),
            pltpu.VMEM((8, 80, 384), bf16),
            pltpu.VMEM((COLS0 * 128, DISP), bf16),
            pltpu.VMEM((COLS1 * 64, DISP), bf16),
            pltpu.VMEM((COLS2 * 64, DISP), bf16),
            pltpu.VMEM((32, DISP), jnp.float32),
            dma((3,)),
            dma((4 * 8,)),
            dma((4, 8)),
            dma((8,)),
            dma((8,)),
            dma((N,)),
            dma,
        ],
        compiler_params=pltpu.CompilerParams(
            collective_id=0, has_side_effects=True, vmem_limit_bytes=56 * 2**20
        ),
        name="stereo",
    )(left_feat, right_feat, w1, w2, w3, head)


def solution(mesh):
    return jax.shard_map(
        shards,
        mesh=mesh,
        in_specs=(P("disp", None, "col"), P("disp", None, "col"), P(), P(), P(), P()),
        out_specs=(P("disp", None, "col"), P(None, "col")),
        check_vma=False,
    )
```

```python
import jax
import jax.numpy as jnp
from jax import lax
from jax.experimental import pallas as pl
from jax.experimental.pallas import tpu as pltpu
from jax.sharding import PartitionSpec as P

N = 16
LANES = 128
DISP = 256
CH_ROWS = 40
SLOT_ROWS = (48, 48, 80, 80)
SLOT_START = (0, 48, 96, 176)
BASE_SHIFT = 14
COLS0, COLS1, COLS2, COLS3 = 22, 20, 18, 16
F = 32
MASKED = -1e30
MESH = pl.DeviceIdType.MESH
NT = (((1,), (1,)), ((), ()))


def first_block(chip):
    return lax.div(chip + 3, 4) - 1


def places(block):
    for low, high, first in ((0, 0, -1), (1, 4, 0), (5, 7, 1)):
        slot = block - first
        if 0 <= slot < 4:
            yield slot, max(low, 3) if slot == 3 and high == 4 else low, high


def dot(a, b, dims=(((1,), (0,)), ((), ()))):
    return lax.dot_general(a, b, dims, preferred_element_type=jnp.float32)


def iota(shape, dim):
    return lax.broadcasted_iota(jnp.int32, shape, dim)


def one_hot(mask):
    return jnp.where(mask, 1.0, 0.0).astype(jnp.bfloat16)


def spread_first(weights, out):
    rows, lane = iota((CH_ROWS, LANES), 0), iota((CH_ROWS, LANES), 1)
    r = lane % 16
    flat = weights[...].reshape(27 * F, CH_ROWS)
    parts = [
        dot(flat, one_hot((rows == lane // 16 * 5 + r // 2) & (r < 10) & (r % 2 == h))) for h in range(2)
    ]
    parts = [part.reshape(3, 3, 3, F, LANES) for part in parts]
    for a in range(3):
        for to in range(2):
            for ho in range(2):
                row = ((a * 2 + to) * 2 + ho) * F
                for ti in range(4):
                    e = ti - to
                    if 0 <= e < 3:
                        block = parts[0][a, 1 - ho, e] + parts[1][a, 2 - ho, e]
                    else:
                        block = jnp.zeros((F, LANES), jnp.float32)
                    out[row : row + F, ti * LANES : (ti + 1) * LANES] = block.astype(jnp.bfloat16)


def spread_later(weights, out):
    rows, lane = iota((F, LANES), 0), iota((F, LANES), 1)
    flat = weights[...].reshape(27 * F, F)
    parts = [dot(flat, one_hot(rows == lane - k * F)).reshape(3, 3, 3, F, LANES) for k in range(4)]
    for a in range(3):
        for to in range(2):
            for ho in range(2):
                row = ((a * 2 + to) * 2 + ho) * F
                for pair in range(2):
                    block = jnp.zeros((F, LANES), jnp.float32)
                    for k in range(4):
                        e, h = pair * 2 + k // 2 - to, k % 2
                        if 0 <= e < 3:
                            block = block + parts[k][a, 1 + h - ho, e]
                    out[row : row + F, pair * LANES : (pair + 1) * LANES] = block.astype(jnp.bfloat16)


def filter_pair(kernel, x):
    taps = dot(kernel, x)
    rows = 2 * 2 * F
    lane = iota((rows, DISP), 1)
    before = jnp.where(lane == DISP - 1, 0.0, pltpu.roll(taps[:rows], DISP - 1, 1))
    after = jnp.where(lane == 0, 0.0, pltpu.roll(taps[2 * rows :], 1, 1))
    return jnp.maximum(taps[rows : 2 * rows] + before + after, 0.0)


def stereo_kernel(
    left_feat, right_feat, w1_hbm, w2_hbm, w3_hbm, head, held,
    right_own, left_own, own, land, parts, w1, w2, w3, k1, k2, k3, right, x0, x1, x2, scores,
    feature_sem, weight_sem, send_sem, recv_sem, pass_send, pass_recv, result_send, result_recv,
):
    i, j = lax.axis_index("disp"), lax.axis_index("col")
    chip, core = lax.div(i, 2), lax.rem(i, 2)
    base = first_block(chip)
    def slot_filled(slot):
        block = 2 * (j - 1) + base + slot
        filled = (block >= 0) & (block < 2 * N)
        if slot == 3:
            filled = filled & ((lax.rem(chip, 4) == 0) | (lax.rem(chip, 4) == 3))
        return filled

    def slot_rows(slot):
        return pl.ds(SLOT_START[slot], SLOT_ROWS[slot])

    barrier = pltpu.get_barrier_semaphore()

    def greet(di, dj):
        pl.semaphore_signal(barrier, inc=1, device_id=(di, dj), device_id_type=MESH)

    def greet_strip(dj):
        @pl.loop(0, 8)
        def _(step):
            greet(2 * lax.rem(chip + step, 8) + core, dj)

    @pl.loop(1, N)
    def _(step):
        greet(lax.rem(i + step, N), j)

    pl.when(j >= 1)(lambda: greet_strip(j - 1))
    pl.when((chip == 0) & (j >= 2))(lambda: greet_strip(j - 2))
    pl.when((chip == 7) & (j <= N - 2))(lambda: greet_strip(j + 1))
    features = ((right_feat, right_own), (left_feat, left_own))
    for n, (src, dst) in enumerate(features):
        pltpu.make_async_copy(src, dst, feature_sem.at[n]).start()
    weights = ((w1_hbm, w1), (w2_hbm, w2), (w3_hbm, w3))
    for n, (src, dst) in enumerate(weights):
        pltpu.make_async_copy(src, dst, weight_sem.at[n]).start()
    for slot in range(4):

        @pl.when(jnp.logical_not(slot_filled(slot)))
        def _(slot=slot):
            for n in range(8):
                land[2 * n + core, slot_rows(slot)] = jnp.zeros((SLOT_ROWS[slot], LANES), jnp.bfloat16)

    head_rows = jnp.where(iota((LANES, F), 0) % F == iota((LANES, F), 1), head[...], 0.0)
    head_column = jnp.sum(head_rows, axis=1, keepdims=True)
    for n, (src, dst) in enumerate(features):
        pltpu.make_async_copy(src, dst, feature_sem.at[n]).wait()
        flat = dst[...].astype(jnp.float32).reshape(CH_ROWS, 256).astype(jnp.bfloat16)
        for half in range(2):
            own[half, n * CH_ROWS : (n + 1) * CH_ROWS] = flat[:, half * LANES : (half + 1) * LANES]

    targets = N - 1 + 8 * (j <= N - 2) + (j <= N - 3) + (j >= 1)
    pl.semaphore_wait(barrier, targets)

    def landing(half, slot):
        return own.at[half, pl.ds(0, SLOT_ROWS[slot])], land.at[i, slot_rows(slot)]

    def copy(go, half, slot, to_chip, dj, sem):
        src, dst = landing(half, slot)
        rdma = pltpu.make_async_remote_copy(
            src_ref=src,
            dst_ref=dst,
            send_sem=send_sem.at[sem],
            recv_sem=recv_sem.at[slot, chip],
            device_id=(2 * to_chip + core, dj),
            device_id_type=MESH,
        )
        rdma.start() if go else rdma.wait_send()

    def push(go, to_chip, dj, half, block, sem):
        for slot, low, high in places(block):

            @pl.when((to_chip >= low) & (to_chip <= high))
            def _(slot=slot):
                copy(go, half, slot, to_chip, dj, sem)

    def exchange(go):
        @pl.loop(0, 8)
        def _(step):
            to_chip = lax.rem(chip + step, 8)

            @pl.when(step > 0)
            def _():
                for half in range(2):
                    push(go, to_chip, j, half, 2 + half, half * 8 + step)

            @pl.when(j <= N - 2)
            def _():
                for half in range(2):
                    push(go, to_chip, j + 1, half, half, (2 + half) * 8 + step)

            @pl.when((to_chip == 0) & (j <= N - 3))
            def _():
                copy(go, 1, 0, to_chip, j + 2, 0)

            @pl.when((to_chip == 7) & (j >= 1))
            def _():
                copy(go, 0, 3, to_chip, j - 1, 8)

    exchange(True)

    for half in range(2):
        for slot, low, high in places(2 + half):

            @pl.when((chip >= low) & (chip <= high))
            def _(half=half, slot=slot):
                pltpu.make_async_copy(*landing(half, slot), recv_sem.at[slot, chip]).start()

    for n, (src, dst) in enumerate(weights):
        pltpu.make_async_copy(src, dst, weight_sem.at[n]).wait()
    spread_first(w1, k1)
    spread_later(w2, k2)
    spread_later(w3, k3)

    start = 16 * i - 2 - BASE_SHIFT - LANES * base
    lane = iota((80, LANES), 1)
    r, lane80 = iota((16, 80), 0), iota((16, 80), 1)
    group_mask = jnp.where((lane80 // 16 == r // 2) & (lane80 % 2 == r % 2), 0.125, 0.0)
    pick = one_hot(iota((32, 2 * LANES), 1) == start + BASE_SHIFT - 1 + iota((32, 2 * LANES), 0))

    def pass_on(s, go):
        held_here = land.at[2 * s + core]
        rdma = pltpu.make_async_remote_copy(
            src_ref=held_here,
            dst_ref=held_here,
            send_sem=pass_send.at[s],
            recv_sem=pass_recv.at[s],
            device_id=(2 * chip + 1 - core, j),
            device_id_type=MESH,
        )
        rdma.start() if go else rdma.wait_send()

    def arrive(n):
        s = lax.rem(chip + 8 - n, 8)
        for slot in range(4):

            @pl.when(slot_filled(slot))
            def _(slot=slot):
                landed = land.at[2 * s + core, slot_rows(slot)]
                pltpu.make_async_copy(landed, landed, recv_sem.at[slot, s]).wait()

        pass_on(s, True)

    for n in range(2):
        arrive(n)

    @pl.loop(0, 8)
    def _(n):
        pl.when(n < 6)(lambda: arrive(n + 2))
        s = lax.rem(chip + 8 - n, 8)
        pair = pl.ds(2 * s, 2)
        passed = land.at[2 * s + 1 - core]
        pltpu.make_async_copy(passed, passed, pass_recv.at[s]).wait()
        blocks = [land[pair, slot_rows(slot)].astype(jnp.float32) for slot in range(4)]
        turned = [
            pltpu.roll(block[:, :CH_ROWS].reshape(80, LANES), LANES - start, 1) for block in blocks
        ]
        moved = [jnp.where(lane < LANES - start, turned[m], turned[m + 1]) for m in range(3)]
        moved = jnp.concatenate(moved, axis=1).astype(jnp.bfloat16)
        right[s] = moved
        left = [block[:, CH_ROWS:].reshape(80, LANES).astype(jnp.bfloat16) for block in blocks[2:]]
        picked = dot(pick[:, :LANES], left[0], NT) + dot(pick[:, LANES:], left[1], NT)
        spread = picked[:COLS0].reshape(COLS0, 1, 80) * group_mask[None]
        spread = spread.reshape(COLS0 * 16, 80).astype(jnp.bfloat16)
        products = dot(spread, moved)
        for k in range(COLS0):
            strip = products[k * 16 : (k + 1) * 16]
            strip = pltpu.roll(strip, 3 * LANES - BASE_SHIFT - k, 1)
            place = pl.ds(pl.multiple_of(k * LANES + s * 16, 16), 16)
            x0[place] = strip[:, :DISP].astype(jnp.bfloat16)

    leftmost, rightmost = (i == 0) & (j == 0), (i == N - 1) & (j == N - 1)
    to = iota((LANES, DISP), 0) // 64
    for p in range(COLS1 // 2):
        y = filter_pair(k1[...], x0[p * 256 : p * 256 + 512])
        if p == 0:
            y = jnp.where(leftmost, 0.0, y)
        if p == COLS1 // 2 - 1:
            y = jnp.where(rightmost, 0.0, y)
        x1[p * LANES : (p + 1) * LANES] = y.astype(jnp.bfloat16)
    for p in range(COLS2 // 2):
        y = filter_pair(k2[...], x1[p * LANES : p * LANES + 256])
        if p == 0:
            y = jnp.where(leftmost & (to == 0), 0.0, y)
        if p == COLS2 // 2 - 1:
            y = jnp.where(rightmost & (to == 1), 0.0, y)
        x2[p * LANES : (p + 1) * LANES] = y.astype(jnp.bfloat16)
    for p in range(COLS3 // 2):
        y = filter_pair(k3[...], x2[p * LANES : p * LANES + 256])
        y = jnp.sum((y * head_column).reshape(4, F, DISP), axis=1)
        for t in range(2):
            for h in range(2):
                row = h * 16 + 2 * p + t
                scores[row : row + 1] = y[2 * t + h : 2 * t + h + 1]

    disp = DISP - 1 - iota((32, DISP), 1)
    column = (N * j + i) * 16 + iota((32, DISP), 0) % 16
    valid = column >= disp
    score = jnp.where(valid, scores[...], MASKED)
    top = jnp.max(score, axis=1, keepdims=True)
    weighting = jnp.where(valid, jnp.exp(score - top), 0.0)
    denominator = jnp.sum(weighting, axis=1, keepdims=True)
    disparity = jnp.sum(weighting * disp.astype(jnp.float32), axis=1, keepdims=True) / denominator / DISP
    padded = jnp.concatenate([weighting, jnp.zeros((32, LANES), jnp.float32)], axis=1)
    band = jnp.concatenate(
        [pltpu.roll(padded[h * 16 : h * 16 + 16], BASE_SHIFT + 3, 1, stride=1, stride_axis=0) for h in range(2)], axis=0
    )
    high = band.astype(jnp.bfloat16)
    low = (band - high.astype(jnp.float32)).astype(jnp.bfloat16)
    band = jnp.concatenate([high, low], axis=0)
    out_lane = iota((16, LANES), 1)
    disp_high = disparity.astype(jnp.bfloat16).astype(jnp.float32)
    disp_low = disparity - disp_high
    tail = jnp.zeros((16, LANES), jnp.float32)
    for n, column_of in enumerate((disp_high[:16], disp_high[16:], disp_low[:16], disp_low[16:])):
        tail = jnp.where(out_lane == 80 + n, column_of, tail)
    even = iota((16, 80), 1) % 2 == 0

    def push_result(di, s, go):
        rdma = pltpu.make_async_remote_copy(
            src_ref=parts.at[s],
            dst_ref=held.at[i],
            send_sem=result_send.at[di],
            recv_sem=result_recv,
            device_id=(di, j),
            device_id_type=MESH,
        )
        rdma.start() if go else rdma.wait_send()

    def each_result(s, go):
        for core in range(2):
            di = 2 * s + core
            pl.when(di != i)(lambda di=di: push_result(di, s, go))

    for s in range(8):
        summed = dot(band, right[s], NT)
        mean = (summed[:32] + summed[32:]) / denominator
        picked = jnp.where(even, mean[:16], mean[16:])
        picked = jnp.concatenate([picked, jnp.zeros((16, LANES - 80), jnp.float32)], axis=1)
        parts[s] = jnp.where(out_lane < 80, picked, tail).astype(jnp.bfloat16)

    pl.loop(0, 8)(lambda n: each_result(lax.rem(chip + 4 + n, 8), True))
    pltpu.make_async_copy(parts.at[chip], held.at[i], result_recv).start()
    exchange(False)
    pl.loop(0, 8)(lambda s: pass_on(s, False))
    pl.loop(0, 8)(lambda s: each_result(s, False))
    pltpu.make_async_copy(held, held, result_recv).wait()


def finish_kernel(held, warped, disparity_out):
    i = lax.axis_index("disp")
    rows, lane = iota((48, LANES), 0), iota((48, LANES), 1)
    mine = lane == lax.rem(i, 2) * CH_ROWS + rows
    extra = (lane == 40 + rows) | (lane == 42 + rows)
    pick = one_hot((mine & (rows < CH_ROWS)) | (extra & (rows >= CH_ROWS) & (rows < CH_ROWS + 2)))
    result = dot(pick, held[...].reshape(256, LANES), NT)
    warped[...] = result[:CH_ROWS].reshape(20, 2, 256).astype(jnp.bfloat16)
    disparity_out[...] = result[CH_ROWS : CH_ROWS + 2]


def shards(left_feat, right_feat, conv1_w, conv2_w, conv3_w, head_w):
    w1, w2, w3 = (jnp.transpose(w, (2, 3, 4, 0, 1)) for w in (conv1_w, conv2_w, conv3_w))
    head = head_w.reshape(1, F)
    vmem, anywhere = pl.BlockSpec(memory_space=pltpu.VMEM), pl.BlockSpec(memory_space=pl.ANY)
    bf16, dma = jnp.bfloat16, pltpu.SemaphoreType.DMA
    held = pl.pallas_call(
        stereo_kernel,
        out_shape=jax.ShapeDtypeStruct((N, 16, LANES), bf16),
        in_specs=[anywhere] * 5 + [vmem],
        out_specs=vmem,
        scratch_shapes=[
            pltpu.VMEM((20, 2, 256), bf16),
            pltpu.VMEM((20, 2, 256), bf16),
            pltpu.VMEM((2, 2 * CH_ROWS, LANES), bf16),
            pltpu.VMEM((N, 256, LANES), bf16),
            pltpu.VMEM((8, 16, LANES), bf16),
            pltpu.VMEM(w1.shape, bf16),
            pltpu.VMEM(w2.shape, bf16),
            pltpu.VMEM(w3.shape, bf16),
            pltpu.VMEM((384, 512), bf16),
            pltpu.VMEM((384, 256), bf16),
            pltpu.VMEM((384, 256), bf16),
            pltpu.VMEM((8, 80, 384), bf16),
            pltpu.VMEM((COLS0 * 128, DISP), bf16),
            pltpu.VMEM((COLS1 * 64, DISP), bf16),
            pltpu.VMEM((COLS2 * 64, DISP), bf16),
            pltpu.VMEM((32, DISP), jnp.float32),
            dma((2,)),
            dma((3,)),
            dma((4 * 8,)),
            dma((4, 8)),
            dma((8,)),
            dma((8,)),
            dma((N,)),
            dma,
        ],
        compiler_params=pltpu.CompilerParams(
            collective_id=0, has_side_effects=True, vmem_limit_bytes=56 * 2**20
        ),
        name="stereo",
    )(left_feat, right_feat, w1, w2, w3, head)
    return pl.pallas_call(
        finish_kernel,
        out_shape=(
            jax.ShapeDtypeStruct((20, 2, 256), bf16),
            jax.ShapeDtypeStruct((2, 256), jnp.float32),
        ),
        in_specs=[vmem],
        out_specs=(vmem, vmem),
        name="finish",
    )(held)


def solution(mesh):
    return jax.shard_map(
        shards,
        mesh=mesh,
        in_specs=(P("disp", None, "col"), P("disp", None, "col"), P(), P(), P(), P()),
        out_specs=(P("disp", None, "col"), P(None, "col")),
        check_vma=False,
    )
```

```python
import jax
import jax.numpy as jnp
from jax import lax
from jax.experimental import pallas as pl
from jax.experimental.pallas import tpu as pltpu
from jax.sharding import PartitionSpec as P

N = 16
LANES = 128
DISP = 256
CH_ROWS = 40
SLOT_ROWS = (48, 48, 80, 80)
SLOT_START = (0, 48, 96, 176)
BASE_SHIFT = 14
COLS0, COLS1, COLS2, COLS3 = 22, 20, 18, 16
F = 32
MASKED = -1e30
MESH = pl.DeviceIdType.MESH
NT = (((1,), (1,)), ((), ()))


def first_block(chip):
    return lax.div(chip + 3, 4) - 1


def places(block):
    for low, high, first in ((0, 0, -1), (1, 4, 0), (5, 7, 1)):
        slot = block - first
        if 0 <= slot < 4:
            yield slot, max(low, 3) if slot == 3 and high == 4 else low, high


def dot(a, b, dims=(((1,), (0,)), ((), ()))):
    return lax.dot_general(a, b, dims, preferred_element_type=jnp.float32)


def iota(shape, dim):
    return lax.broadcasted_iota(jnp.int32, shape, dim)


def one_hot(mask):
    return jnp.where(mask, 1.0, 0.0).astype(jnp.bfloat16)


def spread_first(weights, out):
    rows, lane = iota((CH_ROWS, LANES), 0), iota((CH_ROWS, LANES), 1)
    r = lane % 16
    flat = weights[...].reshape(27 * F, CH_ROWS)
    parts = [
        dot(flat, one_hot((rows == lane // 16 * 5 + r // 2) & (r < 10) & (r % 2 == h))) for h in range(2)
    ]
    parts = [part.reshape(3, 3, 3, F, LANES) for part in parts]
    for a in range(3):
        for to in range(2):
            for ho in range(2):
                row = ((a * 2 + to) * 2 + ho) * F
                for ti in range(4):
                    e = ti - to
                    if 0 <= e < 3:
                        block = parts[0][a, 1 - ho, e] + parts[1][a, 2 - ho, e]
                    else:
                        block = jnp.zeros((F, LANES), jnp.float32)
                    out[row : row + F, ti * LANES : (ti + 1) * LANES] = block.astype(jnp.bfloat16)


def spread_later(weights, out):
    rows, lane = iota((F, LANES), 0), iota((F, LANES), 1)
    flat = weights[...].reshape(27 * F, F)
    parts = [dot(flat, one_hot(rows == lane - k * F)).reshape(3, 3, 3, F, LANES) for k in range(4)]
    for a in range(3):
        for to in range(2):
            for ho in range(2):
                row = ((a * 2 + to) * 2 + ho) * F
                for pair in range(2):
                    block = jnp.zeros((F, LANES), jnp.float32)
                    for k in range(4):
                        e, h = pair * 2 + k // 2 - to, k % 2
                        if 0 <= e < 3:
                            block = block + parts[k][a, 1 + h - ho, e]
                    out[row : row + F, pair * LANES : (pair + 1) * LANES] = block.astype(jnp.bfloat16)


def filter_pair(kernel, x):
    taps = dot(kernel, x)
    rows = 2 * 2 * F
    lane = iota((rows, DISP), 1)
    before = jnp.where(lane == DISP - 1, 0.0, pltpu.roll(taps[:rows], DISP - 1, 1))
    after = jnp.where(lane == 0, 0.0, pltpu.roll(taps[2 * rows :], 1, 1))
    return jnp.maximum(taps[rows : 2 * rows] + before + after, 0.0)


def stereo_kernel(
    left_feat, right_feat, w1_hbm, w2_hbm, w3_hbm, head, held,
    right_own, left_own, own, land, parts, w1, w2, w3, k1, k2, k3, right, x0, x1, x2, scores,
    feature_sem, weight_sem, send_sem, recv_sem, pass_send, pass_recv, result_send, result_recv,
):
    i, j = lax.axis_index("disp"), lax.axis_index("col")
    chip, core = lax.div(i, 2), lax.rem(i, 2)
    base = first_block(chip)
    def slot_filled(slot):
        block = 2 * (j - 1) + base + slot
        filled = (block >= 0) & (block < 2 * N)
        if slot == 3:
            filled = filled & ((lax.rem(chip, 4) == 0) | (lax.rem(chip, 4) == 3))
        return filled

    def slot_rows(slot):
        return pl.ds(SLOT_START[slot], SLOT_ROWS[slot])

    barrier = pltpu.get_barrier_semaphore()

    def greet(di, dj):
        pl.semaphore_signal(barrier, inc=1, device_id=(di, dj), device_id_type=MESH)

    def greet_strip(dj):
        @pl.loop(0, 8)
        def _(step):
            greet(2 * lax.rem(chip + step, 8) + core, dj)

    @pl.loop(1, N)
    def _(step):
        greet(lax.rem(i + step, N), j)

    pl.when(j >= 1)(lambda: greet_strip(j - 1))
    pl.when((chip == 0) & (j >= 2))(lambda: greet_strip(j - 2))
    pl.when((chip == 7) & (j <= N - 2))(lambda: greet_strip(j + 1))
    features = ((right_feat, right_own), (left_feat, left_own))
    for n, (src, dst) in enumerate(features):
        pltpu.make_async_copy(src, dst, feature_sem.at[n]).start()
    weights = ((w1_hbm, w1), (w2_hbm, w2), (w3_hbm, w3))
    for n, (src, dst) in enumerate(weights):
        pltpu.make_async_copy(src, dst, weight_sem.at[n]).start()
    for slot in range(4):

        @pl.when(jnp.logical_not(slot_filled(slot)))
        def _(slot=slot):
            for n in range(8):
                land[2 * n + core, slot_rows(slot)] = jnp.zeros((SLOT_ROWS[slot], LANES), jnp.bfloat16)

    head_rows = jnp.where(iota((LANES, F), 0) % F == iota((LANES, F), 1), head[...], 0.0)
    head_column = jnp.sum(head_rows, axis=1, keepdims=True)
    for n, (src, dst) in enumerate(features):
        pltpu.make_async_copy(src, dst, feature_sem.at[n]).wait()
        flat = dst[...].astype(jnp.float32).reshape(CH_ROWS, 256).astype(jnp.bfloat16)
        for half in range(2):
            own[half, n * CH_ROWS : (n + 1) * CH_ROWS] = flat[:, half * LANES : (half + 1) * LANES]

    for n, (src, dst) in enumerate(weights):
        pltpu.make_async_copy(src, dst, weight_sem.at[n]).wait()
    spread_first(w1, k1)
    spread_later(w2, k2)
    spread_later(w3, k3)

    targets = N - 1 + 8 * (j <= N - 2) + (j <= N - 3) + (j >= 1)
    pl.semaphore_wait(barrier, targets)

    def landing(half, slot):
        return own.at[half, pl.ds(0, SLOT_ROWS[slot])], land.at[i, slot_rows(slot)]

    def copy(go, half, slot, to_chip, dj, sem):
        src, dst = landing(half, slot)
        rdma = pltpu.make_async_remote_copy(
            src_ref=src,
            dst_ref=dst,
            send_sem=send_sem.at[sem],
            recv_sem=recv_sem.at[slot, chip],
            device_id=(2 * to_chip + core, dj),
            device_id_type=MESH,
        )
        rdma.start() if go else rdma.wait_send()

    def push(go, to_chip, dj, half, block, sem):
        for slot, low, high in places(block):

            @pl.when((to_chip >= low) & (to_chip <= high))
            def _(slot=slot):
                copy(go, half, slot, to_chip, dj, sem)

    def exchange(go):
        @pl.loop(0, 8)
        def _(step):
            to_chip = lax.rem(chip + step, 8)

            @pl.when(step > 0)
            def _():
                for half in range(2):
                    push(go, to_chip, j, half, 2 + half, half * 8 + step)

            @pl.when(j <= N - 2)
            def _():
                for half in range(2):
                    push(go, to_chip, j + 1, half, half, (2 + half) * 8 + step)

            @pl.when((to_chip == 0) & (j <= N - 3))
            def _():
                copy(go, 1, 0, to_chip, j + 2, 0)

            @pl.when((to_chip == 7) & (j >= 1))
            def _():
                copy(go, 0, 3, to_chip, j - 1, 8)

    exchange(True)

    for half in range(2):
        for slot, low, high in places(2 + half):

            @pl.when((chip >= low) & (chip <= high))
            def _(half=half, slot=slot):
                pltpu.make_async_copy(*landing(half, slot), recv_sem.at[slot, chip]).start()

    start = 16 * i - 2 - BASE_SHIFT - LANES * base
    lane = iota((80, LANES), 1)
    r, lane80 = iota((16, 80), 0), iota((16, 80), 1)
    group_mask = jnp.where((lane80 // 16 == r // 2) & (lane80 % 2 == r % 2), 0.125, 0.0)
    pick = one_hot(iota((32, 2 * LANES), 1) == start + BASE_SHIFT - 1 + iota((32, 2 * LANES), 0))

    def pass_on(s, go):
        held_here = land.at[2 * s + core]
        rdma = pltpu.make_async_remote_copy(
            src_ref=held_here,
            dst_ref=held_here,
            send_sem=pass_send.at[s],
            recv_sem=pass_recv.at[s],
            device_id=(2 * chip + 1 - core, j),
            device_id_type=MESH,
        )
        rdma.start() if go else rdma.wait_send()

    def arrive(n):
        s = lax.rem(chip + 8 - n, 8)
        for slot in range(4):

            @pl.when(slot_filled(slot))
            def _(slot=slot):
                landed = land.at[2 * s + core, slot_rows(slot)]
                pltpu.make_async_copy(landed, landed, recv_sem.at[slot, s]).wait()

        pass_on(s, True)

    for n in range(2):
        arrive(n)

    @pl.loop(0, 8)
    def _(n):
        pl.when(n < 6)(lambda: arrive(n + 2))
        s = lax.rem(chip + 8 - n, 8)
        pair = pl.ds(2 * s, 2)
        passed = land.at[2 * s + 1 - core]
        pltpu.make_async_copy(passed, passed, pass_recv.at[s]).wait()
        blocks = [land[pair, slot_rows(slot)].astype(jnp.float32) for slot in range(4)]
        turned = [
            pltpu.roll(block[:, :CH_ROWS].reshape(80, LANES), LANES - start, 1) for block in blocks
        ]
        moved = [jnp.where(lane < LANES - start, turned[m], turned[m + 1]) for m in range(3)]
        moved = jnp.concatenate(moved, axis=1).astype(jnp.bfloat16)
        right[s] = moved
        left = [block[:, CH_ROWS:].reshape(80, LANES).astype(jnp.bfloat16) for block in blocks[2:]]
        picked = dot(pick[:, :LANES], left[0], NT) + dot(pick[:, LANES:], left[1], NT)
        spread = picked[:COLS0].reshape(COLS0, 1, 80) * group_mask[None]
        spread = spread.reshape(COLS0 * 16, 80).astype(jnp.bfloat16)
        products = dot(spread, moved)
        for k in range(COLS0):
            strip = products[k * 16 : (k + 1) * 16]
            strip = pltpu.roll(strip, 3 * LANES - BASE_SHIFT - k, 1)
            place = pl.ds(pl.multiple_of(k * LANES + s * 16, 16), 16)
            x0[place] = strip[:, :DISP].astype(jnp.bfloat16)

    leftmost, rightmost = (i == 0) & (j == 0), (i == N - 1) & (j == N - 1)
    to = iota((LANES, DISP), 0) // 64
    for p in range(COLS1 // 2):
        y = filter_pair(k1[...], x0[p * 256 : p * 256 + 512])
        if p == 0:
            y = jnp.where(leftmost, 0.0, y)
        if p == COLS1 // 2 - 1:
            y = jnp.where(rightmost, 0.0, y)
        x1[p * LANES : (p + 1) * LANES] = y.astype(jnp.bfloat16)
    for p in range(COLS2 // 2):
        y = filter_pair(k2[...], x1[p * LANES : p * LANES + 256])
        if p == 0:
            y = jnp.where(leftmost & (to == 0), 0.0, y)
        if p == COLS2 // 2 - 1:
            y = jnp.where(rightmost & (to == 1), 0.0, y)
        x2[p * LANES : (p + 1) * LANES] = y.astype(jnp.bfloat16)
    for p in range(COLS3 // 2):
        y = filter_pair(k3[...], x2[p * LANES : p * LANES + 256])
        y = jnp.sum((y * head_column).reshape(4, F, DISP), axis=1)
        for t in range(2):
            for h in range(2):
                row = h * 16 + 2 * p + t
                scores[row : row + 1] = y[2 * t + h : 2 * t + h + 1]

    disp = DISP - 1 - iota((32, DISP), 1)
    column = (N * j + i) * 16 + iota((32, DISP), 0) % 16
    valid = column >= disp
    score = jnp.where(valid, scores[...], MASKED)
    top = jnp.max(score, axis=1, keepdims=True)
    weighting = jnp.where(valid, jnp.exp(score - top), 0.0)
    denominator = jnp.sum(weighting, axis=1, keepdims=True)
    disparity = jnp.sum(weighting * disp.astype(jnp.float32), axis=1, keepdims=True) / denominator / DISP
    padded = jnp.concatenate([weighting, jnp.zeros((32, LANES), jnp.float32)], axis=1)
    band = jnp.concatenate(
        [pltpu.roll(padded[h * 16 : h * 16 + 16], BASE_SHIFT + 3, 1, stride=1, stride_axis=0) for h in range(2)], axis=0
    )
    high = band.astype(jnp.bfloat16)
    low = (band - high.astype(jnp.float32)).astype(jnp.bfloat16)
    band = jnp.concatenate([high, low], axis=0)
    out_lane = iota((16, LANES), 1)
    disp_high = disparity.astype(jnp.bfloat16).astype(jnp.float32)
    disp_low = disparity - disp_high
    tail = jnp.zeros((16, LANES), jnp.float32)
    for n, column_of in enumerate((disp_high[:16], disp_high[16:], disp_low[:16], disp_low[16:])):
        tail = jnp.where(out_lane == 80 + n, column_of, tail)
    even = iota((16, 80), 1) % 2 == 0

    def push_result(di, s, go):
        rdma = pltpu.make_async_remote_copy(
            src_ref=parts.at[s],
            dst_ref=held.at[i],
            send_sem=result_send.at[di],
            recv_sem=result_recv,
            device_id=(di, j),
            device_id_type=MESH,
        )
        rdma.start() if go else rdma.wait_send()

    def each_result(s, go):
        for core in range(2):
            di = 2 * s + core
            pl.when(di != i)(lambda di=di: push_result(di, s, go))

    for s in range(8):
        summed = dot(band, right[s], NT)
        mean = (summed[:32] + summed[32:]) / denominator
        picked = jnp.where(even, mean[:16], mean[16:])
        picked = jnp.concatenate([picked, jnp.zeros((16, LANES - 80), jnp.float32)], axis=1)
        parts[s] = jnp.where(out_lane < 80, picked, tail).astype(jnp.bfloat16)

    pl.loop(0, 8)(lambda n: each_result(lax.rem(chip + 1 + n, 8), True))
    pltpu.make_async_copy(parts.at[chip], held.at[i], result_recv).start()
    exchange(False)
    pl.loop(0, 8)(lambda s: pass_on(s, False))
    pl.loop(0, 8)(lambda s: each_result(s, False))
    pltpu.make_async_copy(held, held, result_recv).wait()


def finish_kernel(held, warped, disparity_out):
    i = lax.axis_index("disp")
    rows, lane = iota((48, LANES), 0), iota((48, LANES), 1)
    mine = lane == lax.rem(i, 2) * CH_ROWS + rows
    extra = (lane == 40 + rows) | (lane == 42 + rows)
    pick = one_hot((mine & (rows < CH_ROWS)) | (extra & (rows >= CH_ROWS) & (rows < CH_ROWS + 2)))
    result = dot(pick, held[...].reshape(256, LANES), NT)
    warped[...] = result[:CH_ROWS].reshape(20, 2, 256).astype(jnp.bfloat16)
    disparity_out[...] = result[CH_ROWS : CH_ROWS + 2]


def shards(left_feat, right_feat, conv1_w, conv2_w, conv3_w, head_w):
    w1, w2, w3 = (jnp.transpose(w, (2, 3, 4, 0, 1)) for w in (conv1_w, conv2_w, conv3_w))
    head = head_w.reshape(1, F)
    vmem, anywhere = pl.BlockSpec(memory_space=pltpu.VMEM), pl.BlockSpec(memory_space=pl.ANY)
    bf16, dma = jnp.bfloat16, pltpu.SemaphoreType.DMA
    held = pl.pallas_call(
        stereo_kernel,
        out_shape=jax.ShapeDtypeStruct((N, 16, LANES), bf16),
        in_specs=[anywhere] * 5 + [vmem],
        out_specs=vmem,
        scratch_shapes=[
            pltpu.VMEM((20, 2, 256), bf16),
            pltpu.VMEM((20, 2, 256), bf16),
            pltpu.VMEM((2, 2 * CH_ROWS, LANES), bf16),
            pltpu.VMEM((N, 256, LANES), bf16),
            pltpu.VMEM((8, 16, LANES), bf16),
            pltpu.VMEM(w1.shape, bf16),
            pltpu.VMEM(w2.shape, bf16),
            pltpu.VMEM(w3.shape, bf16),
            pltpu.VMEM((384, 512), bf16),
            pltpu.VMEM((384, 256), bf16),
            pltpu.VMEM((384, 256), bf16),
            pltpu.VMEM((8, 80, 384), bf16),
            pltpu.VMEM((COLS0 * 128, DISP), bf16),
            pltpu.VMEM((COLS1 * 64, DISP), bf16),
            pltpu.VMEM((COLS2 * 64, DISP), bf16),
            pltpu.VMEM((32, DISP), jnp.float32),
            dma((2,)),
            dma((3,)),
            dma((4 * 8,)),
            dma((4, 8)),
            dma((8,)),
            dma((8,)),
            dma((N,)),
            dma,
        ],
        compiler_params=pltpu.CompilerParams(
            collective_id=0, has_side_effects=True, vmem_limit_bytes=56 * 2**20
        ),
        name="stereo",
    )(left_feat, right_feat, w1, w2, w3, head)
    return pl.pallas_call(
        finish_kernel,
        out_shape=(
            jax.ShapeDtypeStruct((20, 2, 256), bf16),
            jax.ShapeDtypeStruct((2, 256), jnp.float32),
        ),
        in_specs=[vmem],
        out_specs=(vmem, vmem),
        name="finish",
    )(held)


def solution(mesh):
    return jax.shard_map(
        shards,
        mesh=mesh,
        in_specs=(P("disp", None, "col"), P("disp", None, "col"), P(), P(), P(), P()),
        out_specs=(P("disp", None, "col"), P(None, "col")),
        check_vma=False,
    )
```

```python
import jax
import jax.numpy as jnp
from jax import lax
from jax.experimental import pallas as pl
from jax.experimental.pallas import tpu as pltpu
from jax.sharding import PartitionSpec as P

N = 16
LANES = 128
DISP = 256
CH_ROWS = 40
SLOT_ROWS = (48, 48, 80, 80)
SLOT_START = (0, 48, 96, 176)
BASE_SHIFT = 14
COLS0, COLS1, COLS2, COLS3 = 22, 20, 18, 16
F = 32
MASKED = -1e30
MESH = pl.DeviceIdType.MESH
NT = (((1,), (1,)), ((), ()))


def first_block(chip):
    return lax.div(chip + 3, 4) - 1


def places(block):
    for low, high, first in ((0, 0, -1), (1, 4, 0), (5, 7, 1)):
        slot = block - first
        if 0 <= slot < 4:
            yield slot, max(low, 3) if slot == 3 and high == 4 else low, high


def dot(a, b, dims=(((1,), (0,)), ((), ()))):
    return lax.dot_general(a, b, dims, preferred_element_type=jnp.float32)


def iota(shape, dim):
    return lax.broadcasted_iota(jnp.int32, shape, dim)


def one_hot(mask):
    return jnp.where(mask, 1.0, 0.0).astype(jnp.bfloat16)


def spread_first(weights, out):
    rows, lane = iota((CH_ROWS, LANES), 0), iota((CH_ROWS, LANES), 1)
    r = lane % 16
    flat = weights[...].reshape(27 * F, CH_ROWS)
    parts = [
        dot(flat, one_hot((rows == lane // 16 * 5 + r // 2) & (r < 10) & (r % 2 == h))) for h in range(2)
    ]
    parts = [part.reshape(3, 3, 3, F, LANES) for part in parts]
    for a in range(3):
        for to in range(2):
            for ho in range(2):
                row = ((a * 2 + to) * 2 + ho) * F
                for ti in range(4):
                    e = ti - to
                    if 0 <= e < 3:
                        block = parts[0][a, 1 - ho, e] + parts[1][a, 2 - ho, e]
                    else:
                        block = jnp.zeros((F, LANES), jnp.float32)
                    out[row : row + F, ti * LANES : (ti + 1) * LANES] = block.astype(jnp.bfloat16)


def spread_later(weights, out):
    rows, lane = iota((F, LANES), 0), iota((F, LANES), 1)
    flat = weights[...].reshape(27 * F, F)
    parts = [dot(flat, one_hot(rows == lane - k * F)).reshape(3, 3, 3, F, LANES) for k in range(4)]
    for a in range(3):
        for to in range(2):
            for ho in range(2):
                row = ((a * 2 + to) * 2 + ho) * F
                for pair in range(2):
                    block = jnp.zeros((F, LANES), jnp.float32)
                    for k in range(4):
                        e, h = pair * 2 + k // 2 - to, k % 2
                        if 0 <= e < 3:
                            block = block + parts[k][a, 1 + h - ho, e]
                    out[row : row + F, pair * LANES : (pair + 1) * LANES] = block.astype(jnp.bfloat16)


def filter_pair(kernel, x):
    taps = dot(kernel, x)
    rows = 2 * 2 * F
    lane = iota((rows, DISP), 1)
    before = jnp.where(lane == DISP - 1, 0.0, pltpu.roll(taps[:rows], DISP - 1, 1))
    after = jnp.where(lane == 0, 0.0, pltpu.roll(taps[2 * rows :], 1, 1))
    return jnp.maximum(taps[rows : 2 * rows] + before + after, 0.0)


def stereo_kernel(
    left_feat, right_feat, w1_hbm, w2_hbm, w3_hbm, head, held,
    right_own, left_own, own, land, parts, w1, w2, w3, k1, k2, k3, right, x0, x1, x2, scores,
    feature_sem, weight_sem, send_sem, recv_sem, pass_send, pass_recv, result_send, result_recv,
):
    i, j = lax.axis_index("disp"), lax.axis_index("col")
    chip, core = lax.div(i, 2), lax.rem(i, 2)
    base = first_block(chip)
    def slot_filled(slot):
        block = 2 * (j - 1) + base + slot
        filled = (block >= 0) & (block < 2 * N)
        if slot == 3:
            filled = filled & ((lax.rem(chip, 4) == 0) | (lax.rem(chip, 4) == 3))
        return filled

    def slot_rows(slot):
        return pl.ds(SLOT_START[slot], SLOT_ROWS[slot])

    barrier = pltpu.get_barrier_semaphore()

    def greet(di, dj):
        pl.semaphore_signal(barrier, inc=1, device_id=(di, dj), device_id_type=MESH)

    def greet_strip(dj):
        @pl.loop(0, 8)
        def _(step):
            greet(2 * lax.rem(chip + step, 8) + core, dj)

    @pl.loop(1, N)
    def _(step):
        greet(lax.rem(i + step, N), j)

    pl.when(j >= 1)(lambda: greet_strip(j - 1))
    pl.when((chip == 0) & (j >= 2))(lambda: greet_strip(j - 2))
    pl.when((chip == 7) & (j <= N - 2))(lambda: greet_strip(j + 1))
    features = ((right_feat, right_own), (left_feat, left_own))
    for n, (src, dst) in enumerate(features):
        pltpu.make_async_copy(src, dst, feature_sem.at[n]).start()
    weights = ((w1_hbm, w1), (w2_hbm, w2), (w3_hbm, w3))
    for n, (src, dst) in enumerate(weights):
        pltpu.make_async_copy(src, dst, weight_sem.at[n]).start()
    for slot in range(4):

        @pl.when(jnp.logical_not(slot_filled(slot)))
        def _(slot=slot):
            for n in range(8):
                land[2 * n + core, slot_rows(slot)] = jnp.zeros((SLOT_ROWS[slot], LANES), jnp.bfloat16)

    head_rows = jnp.where(iota((LANES, F), 0) % F == iota((LANES, F), 1), head[...], 0.0)
    head_column = jnp.sum(head_rows, axis=1, keepdims=True)
    for n, (src, dst) in enumerate(features):
        pltpu.make_async_copy(src, dst, feature_sem.at[n]).wait()
        flat = dst[...].astype(jnp.float32).reshape(CH_ROWS, 256).astype(jnp.bfloat16)
        for half in range(2):
            own[half, n * CH_ROWS : (n + 1) * CH_ROWS] = flat[:, half * LANES : (half + 1) * LANES]

    for n, (src, dst) in enumerate(weights):
        pltpu.make_async_copy(src, dst, weight_sem.at[n]).wait()
    spread_first(w1, k1)
    spread_later(w2, k2)
    spread_later(w3, k3)

    targets = N - 1 + 8 * (j <= N - 2) + (j <= N - 3) + (j >= 1)
    pl.semaphore_wait(barrier, targets)

    def landing(half, slot):
        return own.at[half, pl.ds(0, SLOT_ROWS[slot])], land.at[i, slot_rows(slot)]

    def copy(go, half, slot, to_chip, dj, sem):
        src, dst = landing(half, slot)
        rdma = pltpu.make_async_remote_copy(
            src_ref=src,
            dst_ref=dst,
            send_sem=send_sem.at[sem],
            recv_sem=recv_sem.at[slot, chip],
            device_id=(2 * to_chip + core, dj),
            device_id_type=MESH,
        )
        rdma.start() if go else rdma.wait_send()

    def push(go, to_chip, dj, half, block, sem):
        for slot, low, high in places(block):

            @pl.when((to_chip >= low) & (to_chip <= high))
            def _(slot=slot):
                copy(go, half, slot, to_chip, dj, sem)

    def exchange(go):
        @pl.loop(0, 8)
        def _(step):
            to_chip = lax.rem(chip + step, 8)

            @pl.when(step > 0)
            def _():
                for half in range(2):
                    push(go, to_chip, j, half, 2 + half, half * 8 + step)

            @pl.when(j <= N - 2)
            def _():
                for half in range(2):
                    push(go, to_chip, j + 1, half, half, (2 + half) * 8 + step)

            @pl.when((to_chip == 0) & (j <= N - 3))
            def _():
                copy(go, 1, 0, to_chip, j + 2, 0)

            @pl.when((to_chip == 7) & (j >= 1))
            def _():
                copy(go, 0, 3, to_chip, j - 1, 8)

    exchange(True)

    for half in range(2):
        for slot, low, high in places(2 + half):

            @pl.when((chip >= low) & (chip <= high))
            def _(half=half, slot=slot):
                pltpu.make_async_copy(*landing(half, slot), recv_sem.at[slot, chip]).start()

    start = 16 * i - 2 - BASE_SHIFT - LANES * base
    lane = iota((80, LANES), 1)
    r, lane80 = iota((16, 80), 0), iota((16, 80), 1)
    group_mask = jnp.where((lane80 // 16 == r // 2) & (lane80 % 2 == r % 2), 0.125, 0.0)
    pick = one_hot(iota((32, 2 * LANES), 1) == start + BASE_SHIFT - 1 + iota((32, 2 * LANES), 0))

    def pass_on(s, go):
        held_here = land.at[2 * s + core]
        rdma = pltpu.make_async_remote_copy(
            src_ref=held_here,
            dst_ref=held_here,
            send_sem=pass_send.at[s],
            recv_sem=pass_recv.at[s],
            device_id=(2 * chip + 1 - core, j),
            device_id_type=MESH,
        )
        rdma.start() if go else rdma.wait_send()

    def arrive(n):
        s = lax.rem(chip + 8 - n, 8)
        for slot in range(4):

            @pl.when(slot_filled(slot))
            def _(slot=slot):
                landed = land.at[2 * s + core, slot_rows(slot)]
                pltpu.make_async_copy(landed, landed, recv_sem.at[slot, s]).wait()

        pass_on(s, True)

    for n in range(2):
        arrive(n)

    @pl.loop(0, 8)
    def _(n):
        s = lax.rem(chip + 8 - n, 8)
        pair = pl.ds(2 * s, 2)
        passed = land.at[2 * s + 1 - core]
        pltpu.make_async_copy(passed, passed, pass_recv.at[s]).wait()
        blocks = [land[pair, slot_rows(slot)].astype(jnp.float32) for slot in range(4)]
        turned = [
            pltpu.roll(block[:, :CH_ROWS].reshape(80, LANES), LANES - start, 1) for block in blocks
        ]
        moved = [jnp.where(lane < LANES - start, turned[m], turned[m + 1]) for m in range(3)]
        moved = jnp.concatenate(moved, axis=1).astype(jnp.bfloat16)
        right[s] = moved
        left = [block[:, CH_ROWS:].reshape(80, LANES).astype(jnp.bfloat16) for block in blocks[2:]]
        picked = dot(pick[:, :LANES], left[0], NT) + dot(pick[:, LANES:], left[1], NT)
        spread = picked[:COLS0].reshape(COLS0, 1, 80) * group_mask[None]
        spread = spread.reshape(COLS0 * 16, 80).astype(jnp.bfloat16)
        products = dot(spread, moved)
        for k in range(COLS0):
            strip = products[k * 16 : (k + 1) * 16]
            strip = pltpu.roll(strip, 3 * LANES - BASE_SHIFT - k, 1)
            place = pl.ds(pl.multiple_of(k * LANES + s * 16, 16), 16)
            x0[place] = strip[:, :DISP].astype(jnp.bfloat16)

        pl.when(n < 6)(lambda: arrive(n + 2))

    leftmost, rightmost = (i == 0) & (j == 0), (i == N - 1) & (j == N - 1)
    to = iota((LANES, DISP), 0) // 64
    for p in range(COLS1 // 2):
        y = filter_pair(k1[...], x0[p * 256 : p * 256 + 512])
        if p == 0:
            y = jnp.where(leftmost, 0.0, y)
        if p == COLS1 // 2 - 1:
            y = jnp.where(rightmost, 0.0, y)
        x1[p * LANES : (p + 1) * LANES] = y.astype(jnp.bfloat16)
    for p in range(COLS2 // 2):
        y = filter_pair(k2[...], x1[p * LANES : p * LANES + 256])
        if p == 0:
            y = jnp.where(leftmost & (to == 0), 0.0, y)
        if p == COLS2 // 2 - 1:
            y = jnp.where(rightmost & (to == 1), 0.0, y)
        x2[p * LANES : (p + 1) * LANES] = y.astype(jnp.bfloat16)
    for p in range(COLS3 // 2):
        y = filter_pair(k3[...], x2[p * LANES : p * LANES + 256])
        y = jnp.sum((y * head_column).reshape(4, F, DISP), axis=1)
        for t in range(2):
            for h in range(2):
                row = h * 16 + 2 * p + t
                scores[row : row + 1] = y[2 * t + h : 2 * t + h + 1]

    disp = DISP - 1 - iota((32, DISP), 1)
    column = (N * j + i) * 16 + iota((32, DISP), 0) % 16
    valid = column >= disp
    score = jnp.where(valid, scores[...], MASKED)
    top = jnp.max(score, axis=1, keepdims=True)
    weighting = jnp.where(valid, jnp.exp(score - top), 0.0)
    denominator = jnp.sum(weighting, axis=1, keepdims=True)
    disparity = jnp.sum(weighting * disp.astype(jnp.float32), axis=1, keepdims=True) / denominator / DISP
    padded = jnp.concatenate([weighting, jnp.zeros((32, LANES), jnp.float32)], axis=1)
    band = jnp.concatenate(
        [pltpu.roll(padded[h * 16 : h * 16 + 16], BASE_SHIFT + 3, 1, stride=1, stride_axis=0) for h in range(2)], axis=0
    )
    high = band.astype(jnp.bfloat16)
    low = (band - high.astype(jnp.float32)).astype(jnp.bfloat16)
    band = jnp.concatenate([high, low], axis=0)
    out_lane = iota((16, LANES), 1)
    disp_high = disparity.astype(jnp.bfloat16).astype(jnp.float32)
    disp_low = disparity - disp_high
    tail = jnp.zeros((16, LANES), jnp.float32)
    for n, column_of in enumerate((disp_high[:16], disp_high[16:], disp_low[:16], disp_low[16:])):
        tail = jnp.where(out_lane == 80 + n, column_of, tail)
    even = iota((16, 80), 1) % 2 == 0

    def push_result(di, s, go):
        rdma = pltpu.make_async_remote_copy(
            src_ref=parts.at[s],
            dst_ref=held.at[i],
            send_sem=result_send.at[di],
            recv_sem=result_recv,
            device_id=(di, j),
            device_id_type=MESH,
        )
        rdma.start() if go else rdma.wait_send()

    def each_result(s, go):
        for core in range(2):
            di = 2 * s + core
            pl.when(di != i)(lambda di=di: push_result(di, s, go))

    for s in range(8):
        summed = dot(band, right[s], NT)
        mean = (summed[:32] + summed[32:]) / denominator
        picked = jnp.where(even, mean[:16], mean[16:])
        picked = jnp.concatenate([picked, jnp.zeros((16, LANES - 80), jnp.float32)], axis=1)
        parts[s] = jnp.where(out_lane < 80, picked, tail).astype(jnp.bfloat16)

    pl.loop(0, 8)(lambda n: each_result(lax.rem(chip + 1 + n, 8), True))
    pltpu.make_async_copy(parts.at[chip], held.at[i], result_recv).start()
    exchange(False)
    pl.loop(0, 8)(lambda s: pass_on(s, False))
    pl.loop(0, 8)(lambda s: each_result(s, False))
    pltpu.make_async_copy(held, held, result_recv).wait()


def finish_kernel(held, warped, disparity_out):
    i = lax.axis_index("disp")
    rows, lane = iota((48, LANES), 0), iota((48, LANES), 1)
    mine = lane == lax.rem(i, 2) * CH_ROWS + rows
    extra = (lane == 40 + rows) | (lane == 42 + rows)
    pick = one_hot((mine & (rows < CH_ROWS)) | (extra & (rows >= CH_ROWS) & (rows < CH_ROWS + 2)))
    result = dot(pick, held[...].reshape(256, LANES), NT)
    warped[...] = result[:CH_ROWS].reshape(20, 2, 256).astype(jnp.bfloat16)
    disparity_out[...] = result[CH_ROWS : CH_ROWS + 2]


def shards(left_feat, right_feat, conv1_w, conv2_w, conv3_w, head_w):
    w1, w2, w3 = (jnp.transpose(w, (2, 3, 4, 0, 1)) for w in (conv1_w, conv2_w, conv3_w))
    head = head_w.reshape(1, F)
    vmem, anywhere = pl.BlockSpec(memory_space=pltpu.VMEM), pl.BlockSpec(memory_space=pl.ANY)
    bf16, dma = jnp.bfloat16, pltpu.SemaphoreType.DMA
    held = pl.pallas_call(
        stereo_kernel,
        out_shape=jax.ShapeDtypeStruct((N, 16, LANES), bf16),
        in_specs=[anywhere] * 5 + [vmem],
        out_specs=vmem,
        scratch_shapes=[
            pltpu.VMEM((20, 2, 256), bf16),
            pltpu.VMEM((20, 2, 256), bf16),
            pltpu.VMEM((2, 2 * CH_ROWS, LANES), bf16),
            pltpu.VMEM((N, 256, LANES), bf16),
            pltpu.VMEM((8, 16, LANES), bf16),
            pltpu.VMEM(w1.shape, bf16),
            pltpu.VMEM(w2.shape, bf16),
            pltpu.VMEM(w3.shape, bf16),
            pltpu.VMEM((384, 512), bf16),
            pltpu.VMEM((384, 256), bf16),
            pltpu.VMEM((384, 256), bf16),
            pltpu.VMEM((8, 80, 384), bf16),
            pltpu.VMEM((COLS0 * 128, DISP), bf16),
            pltpu.VMEM((COLS1 * 64, DISP), bf16),
            pltpu.VMEM((COLS2 * 64, DISP), bf16),
            pltpu.VMEM((32, DISP), jnp.float32),
            dma((2,)),
            dma((3,)),
            dma((4 * 8,)),
            dma((4, 8)),
            dma((8,)),
            dma((8,)),
            dma((N,)),
            dma,
        ],
        compiler_params=pltpu.CompilerParams(
            collective_id=0, has_side_effects=True, vmem_limit_bytes=56 * 2**20
        ),
        name="stereo",
    )(left_feat, right_feat, w1, w2, w3, head)
    return pl.pallas_call(
        finish_kernel,
        out_shape=(
            jax.ShapeDtypeStruct((20, 2, 256), bf16),
            jax.ShapeDtypeStruct((2, 256), jnp.float32),
        ),
        in_specs=[vmem],
        out_specs=(vmem, vmem),
        name="finish",
    )(held)


def solution(mesh):
    return jax.shard_map(
        shards,
        mesh=mesh,
        in_specs=(P("disp", None, "col"), P("disp", None, "col"), P(), P(), P(), P()),
        out_specs=(P("disp", None, "col"), P(None, "col")),
        check_vma=False,
    )
```
